32 devices in a mesh: rows: 4 (over y, x), cols: 8 (over z, core).
Axes of the slice: x: 2, y: 2, z: 4, core: 2. Of those that a mesh axis runs over, the one named last changes fastest.
Arguments:
- power: float32 [2, 4, 512, 1024], P(None, None, 'rows', 'cols'), may hold values from -6 to 6
- material: int32 [4, 512, 1024], P(None, 'rows', 'cols'), may hold values from 0 to 7
- cond_table: float32 [4, 8], replicated, may hold values from 0.5 to 8
- tier_table: int32 [4], replicated, may hold values from 0 to 3
- coarse_slot: int32 [32], replicated, may hold values from 0 to 31, each once
- coarse_inverse: float32 [8, 4, 4], replicated, as said below
Outputs:
- solution: float32 [2, 4, 512, 1024], P(None, None, 'rows', 'cols')
- residual: float32 [2, 4, 512, 1024], P(None, None, 'rows', 'cols')
- precond: float32 [2, 4, 512, 1024], P(None, None, 'rows', 'cols')
The draws below stay inside these ranges and needn't reach their ends.
Inputs may be any that keep to these rules, and one draw needn't show every extreme that they name: `coarse_slot`: each value once. `coarse_inverse`: symmetric within each owner.
All inputs are finite; a program needn't handle non-finite values.
Results may differ from the reference program's by a relative error of at most 0.0003.
Values sent between devices are 32-bit elements; how exact they have to be, the bound alone decides.
A program may use at most 64 MiB of HBM per device.

```python
import math
import jax
import jax.numpy as jnp
from jax import lax

SUB = 128
VARIANTS = 2
TIERS = 4
MATS = 8
TABLES = 4
ITERS = 2
NX = 512
NY = 1024
COARSE = 32
OWNERS = 8
OWN = 4


def draw_power(key, part):
    shape = (VARIANTS, TIERS, NX, NY)
    values = jnp.clip(jax.random.normal(key, shape, jnp.float32), -6.0, 6.0)
    return values


def draw_coarse_inverse(key, part):
    draw_key, spare_key = jax.random.split(jax.random.fold_in(key, 7))
    shape = (OWNERS, OWN, OWN)
    uniform_part = jax.random.uniform(draw_key, shape, jnp.float32, -1.0, 1.0)
    symmetric = 0.5 * (uniform_part + jnp.swapaxes(uniform_part, 1, 2)) * (12.0 / OWN)
    identity = jnp.eye(OWN, dtype=jnp.float32)[None, :, :]
    diagonal = jax.random.uniform(spare_key, shape, jnp.float32, 14.0, 30.0)
    return symmetric * (1.0 - identity) + diagonal * identity


def plant(array, key, least, top_value):
    longest = array.shape.index(max(array.shape))
    spots = []
    for shift in (0, 1):
        where = [jax.random.randint(jax.random.fold_in(key, axis), (), 0, length) for axis, length in enumerate(array.shape)]
        where[longest] = (where[longest] + shift) % array.shape[longest]
        spots.append(tuple(where))
    return array.at[spots[0]].set(least).at[spots[1]].set(top_value)


def setup_inputs(seed: int = 0) -> dict:
    seeds = jax.random.split(jax.random.key(seed), 7)
    return {
        "power": draw_power(jax.random.fold_in(seeds[6], 71), 0),
        "material": plant(jax.random.randint(seeds[1], (TIERS, NX, NY), 0, MATS), jax.random.fold_in(seeds[1], 1), 0, MATS - 1).astype(jnp.int32),
        "cond_table": jnp.clip(jnp.exp(jax.random.uniform(seeds[2], (TABLES, MATS), jnp.float32, math.log(0.5), math.log(8.0))), 0.5, 8.0),
        "tier_table": plant(jax.random.randint(seeds[3], (TIERS,), 0, TABLES), jax.random.fold_in(seeds[3], 1), 0, TABLES - 1).astype(jnp.int32),
        "coarse_slot": jax.random.permutation(seeds[4], COARSE).astype(jnp.int32),
        "coarse_inverse": draw_coarse_inverse(jax.random.fold_in(seeds[6], 71), 0),
    }


SHIFT_C = 0.5
VERT_C = 2.0
SINK_C = 0.05
HIGH = lax.Precision.HIGHEST

def sine_basis(length):
    counting = jnp.arange(1, length + 1).astype(jnp.float32)
    step_angle = math.pi / (length + 1)
    basis = math.sqrt(2.0 / (length + 1)) * jnp.sin(step_angle * counting[:, None] * counting[None, :])
    eigen_values = 2.0 - 2.0 * jnp.cos(step_angle * counting)
    return (basis, eigen_values)

def conductivity(material, cond_table, tier_table):
    tables = cond_table.shape[0]
    picker = (tier_table[:, None] == jnp.arange(tables, dtype=jnp.int32)[None, :]).astype(jnp.float32)
    tier_rows = jnp.dot(picker, cond_table, precision=HIGH)
    cond = jnp.zeros(material.shape, jnp.float32)
    for number in range(cond_table.shape[1]):
        cond = cond + jnp.where(material == number, tier_rows[:, number][:, None, None], 0.0)
    return (cond, lax.optimization_barrier(jnp.mean(tier_rows, axis=1)))

def coefficients(cond, padded):
    north = 0.5 * (cond + padded[:, :-2, 1:-1])
    south = 0.5 * (cond + padded[:, 2:, 1:-1])
    west = 0.5 * (cond + padded[:, 1:-1, :-2])
    east = 0.5 * (cond + padded[:, 1:-1, 2:])
    upward = VERT_C * 0.5 * (cond[:-1] + cond[1:])
    sink = jnp.concatenate([SINK_C * cond[:1], jnp.zeros_like(cond[1:])], 0)
    return (north, south, west, east, upward, sink)

def operate(temps, padded, coefs):
    north, south, west, east, upward, sink = coefs
    lateral = north * (temps - padded[:, :, :-2, 1:-1]) + south * (temps - padded[:, :, 2:, 1:-1])
    lateral = lateral + west * (temps - padded[:, :, 1:-1, :-2]) + east * (temps - padded[:, :, 1:-1, 2:])
    flux = upward * (temps[:, :-1] - temps[:, 1:])
    zeros_tier = jnp.zeros_like(temps[:, :1])
    vertical = jnp.concatenate([flux, zeros_tier], 1) - jnp.concatenate([zeros_tier, flux], 1)
    return lateral + vertical + sink * temps

def block_solve(temps, basis, denominator):
    shape = temps.shape
    length = basis.shape[0]
    blocks = temps.reshape(shape[0], shape[1], shape[2] // length, length, shape[3] // length, length)
    spectral = jnp.einsum('ia,vtxayb->vtxiyb', basis, blocks, precision=HIGH)
    spectral = jnp.einsum('vtxiyb,bj->vtxiyj', spectral, basis, precision=HIGH)
    spectral = spectral / denominator[None, :, None, :, None, :]
    result = jnp.einsum('ia,vtxayb->vtxiyb', basis, spectral, precision=HIGH)
    result = jnp.einsum('vtxiyb,bj->vtxiyj', result, basis, precision=HIGH)
    return result.reshape(shape)

def reference(power, material, cond_table, tier_table, coarse_slot, coarse_inverse):
    cond, mean_cond = conductivity(material, cond_table, tier_table)
    coefs = coefficients(cond, jnp.pad(cond, ((0, 0), (1, 1), (1, 1))))
    basis, eigen_values = sine_basis(SUB)
    denominator = mean_cond[:, None, None] * (eigen_values[:, None] + eigen_values[None, :] + SHIFT_C)
    half = SUB // 2
    scale = 1.0 / math.sqrt(SUB * SUB * TIERS)

    def apply_a(temps):
        return operate(temps, jnp.pad(temps, ((0, 0), (0, 0), (1, 1), (1, 1))), coefs)

    def precondition(resid):
        aligned = block_solve(resid, basis, denominator)
        moved = jnp.pad(resid, ((0, 0), (0, 0), (0, half), (0, half)))[:, :, half:, half:]
        offset = block_solve(moved, basis, denominator)
        offset = jnp.pad(offset, ((0, 0), (0, 0), (half, 0), (half, 0)))[:, :, :NX, :NY]
        sums = resid.reshape(VARIANTS, TIERS, NX // SUB, SUB, NY // SUB, SUB).sum(axis=(1, 3, 5)) * scale
        ordered = jnp.zeros((COARSE, VARIANTS), jnp.float32).at[coarse_slot].set(sums.reshape(VARIANTS, COARSE).T)
        solved = jnp.einsum('okj,ojv->okv', coarse_inverse, ordered.reshape(OWNERS, OWN, VARIANTS), precision=HIGH)
        picked = solved.reshape(COARSE, VARIANTS)[coarse_slot].T.reshape(VARIANTS, NX // SUB, NY // SUB)
        coarse = jnp.broadcast_to(picked[:, None, :, None, :, None], (VARIANTS, TIERS, NX // SUB, SUB, NY // SUB, SUB))
        return aligned + offset + coarse.reshape(resid.shape) * scale
    solution = jnp.zeros_like(power)
    residual = power
    precond = precondition(residual)
    direction = precond
    rz_now = lax.optimization_barrier(jnp.sum(residual * precond, axis=(1, 2, 3)))
    for number in range(ITERS):
        image = apply_a(direction)
        alpha = rz_now / lax.optimization_barrier(jnp.sum(direction * image, axis=(1, 2, 3)))
        solution = solution + alpha[:, None, None, None] * direction
        residual = residual - alpha[:, None, None, None] * image
        precond = precondition(residual)
        rz_next = lax.optimization_barrier(jnp.sum(residual * precond, axis=(1, 2, 3)))
        direction = precond + (rz_next / rz_now)[:, None, None, None] * direction
        rz_now = rz_next
    return (solution, residual, precond)
```

```python
import math

import jax
import jax.numpy as jnp
import numpy as np
from jax import lax
from jax.experimental import pallas as pl
from jax.experimental.pallas import tpu as pltpu
from jax.sharding import PartitionSpec as P

SUB = 128
HALF = SUB // 2
TIERS = 4
ITERS = 2

SHIFT_C = 0.5
VERT_C = 2.0
SINK_C = 0.05
MESH = pl.DeviceIdType.MESH


def split_constants():
    counting = np.arange(1, SUB + 1)
    angle = np.pi / (SUB + 1)
    product = (counting[:, None] * counting[None, :]) % (2 * (SUB + 1))
    basis = np.sqrt(2.0 / (SUB + 1)) * np.sin(angle * product)
    eigen = 2.0 - 2.0 * np.cos(angle * counting)
    recip = 1.0 / (eigen[:, None] + eigen[None, :] + SHIFT_C)
    rolled = np.roll(basis, HALF, axis=0)
    rights, lefts = [], []
    for matrix in (basis, rolled, rolled.T):
        high = matrix.astype(np.float32).astype(jnp.bfloat16)
        low = (matrix - high.astype(np.float64)).astype(np.float32).astype(jnp.bfloat16)
        wide = np.concatenate([high, low], 1)
        rights.append(np.concatenate([wide, wide], 0))
        tall = np.concatenate([high, low], 0)
        lefts.append(np.concatenate([tall, tall], 1))
    return np.stack(rights), np.stack(lefts), recip.astype(np.float32)


def halves(value):
    high = value.astype(jnp.bfloat16)
    low = (value - high.astype(jnp.float32)).astype(jnp.bfloat16)
    return high, low


def kernel(
    rows, cols, variants, owners, own,
    power, material, rights, lefts, recip, cond_table, tier_table, slots, inverse,
    sol, res, pre,
    inv_den, coef, upward, sink, held, image, held_image,
    fwd_send, fwd_recv, back_send, back_recv,
    row_send, row_recv, col_send, col_recv, gather_cols, gather_rows,
    send_sem, recv_sem,
):
    i, j = lax.axis_index("rows"), lax.axis_index("cols")
    not_first_row, not_last_row = i > 0, i < rows - 1
    not_first_col, not_last_col = j > 0, j < cols - 1
    up, down = jnp.maximum(i - 1, 0), jnp.minimum(i + 1, rows - 1)
    before, after = jnp.maximum(j - 1, 0), jnp.minimum(j + 1, cols - 1)
    scale = 1.0 / math.sqrt(SUB * SUB * TIERS)

    barrier = pltpu.get_barrier_semaphore()
    for step in range(1, cols):
        pl.semaphore_signal(
            barrier, 1, device_id=(i, lax.rem(j + step, cols)), device_id_type=MESH
        )
    for step in range(1, rows):
        pl.semaphore_signal(
            barrier, 1, device_id=(lax.rem(i + step, rows), j), device_id_type=MESH
        )
    to_front = jnp.logical_and(not_first_row, not_first_col)
    to_back = jnp.logical_and(not_last_row, not_last_col)

    @pl.when(to_front)
    def _():
        pl.semaphore_signal(barrier, 1, device_id=(up, before), device_id_type=MESH)

    @pl.when(to_back)
    def _():
        pl.semaphore_signal(barrier, 1, device_id=(down, after), device_id_type=MESH)

    fwd_route = (
        ((up, before), to_front, to_back),
        ((up, j), not_first_row, not_last_row),
        ((i, before), not_first_col, not_last_col),
    )
    back_route = (
        ((down, after), to_back, to_front),
        ((down, j), not_last_row, not_first_row),
        ((i, after), not_last_col, not_first_col),
    )
    quads = ((0, 0), (0, 1), (1, 0))
    counter = [0]
    pending = []

    def message(source, target, device, may_send):
        number = counter[0]
        counter[0] += 1
        copy = pltpu.make_async_remote_copy(
            source, target, send_sem.at[number], recv_sem.at[number],
            device_id=device, device_id_type=MESH,
        )
        if may_send is None:
            copy.start()
        else:
            pl.when(may_send)(lambda: copy.start())
        pending.append((copy, may_send))
        return copy

    def receive(copy, may_receive):
        if may_receive is None:
            copy.wait_recv()
        else:
            pl.when(may_receive)(lambda: copy.wait_recv())

    lane = lax.broadcasted_iota(jnp.int32, (HALF, SUB), 1)
    is_left = lane < HALF
    full_lane = lax.broadcasted_iota(jnp.int32, (SUB, SUB), 1)
    full_row = lax.broadcasted_iota(jnp.int32, (SUB, SUB), 0)
    tile_lane = lax.broadcasted_iota(jnp.int32, (8, SUB), 1)

    def swap(value):
        return pltpu.roll(value, HALF, 1)

    def send_quads(tiles, sender, receiver, route, apply, v):
        copies = []
        for q, (low, right) in enumerate(quads):
            span = slice(low * HALF, (low + 1) * HALF)
            for pair in range(TIERS // 2):
                first, second = tiles[pair][span], tiles[pair + TIERS // 2][span]
                if right:
                    packed = jnp.where(is_left, swap(first), second)
                else:
                    packed = jnp.where(is_left, first, swap(second))
                sender[apply, v, q, pair] = packed
            device, may_send, may_receive = route[q]
            copy = message(
                sender.at[apply, v, q], receiver.at[apply, v, q], device, may_send
            )
            copies.append((copy, may_receive))
        return copies

    def quad_halves(receiver, apply, v, t):
        pair, second = t % (TIERS // 2), t >= TIERS // 2
        top_left = receiver[apply, v, 0, pair]
        top_right = receiver[apply, v, 1, pair]
        low_left = receiver[apply, v, 2, pair]
        if second:
            top_left, low_left = swap(top_left), swap(low_left)
        else:
            top_right = swap(top_right)
        return jnp.where(is_left, top_left, top_right), low_left

    def right_mul(value, which):
        high, low = halves(value)
        wide = jnp.dot(
            jnp.concatenate([high, low], 1), rights[which], preferred_element_type=jnp.float32
        )
        return wide[:, :SUB] + wide[:, SUB:]

    def left_mul(value, which):
        high, low = halves(value)
        tall = jnp.dot(
            lefts[which], jnp.concatenate([high, low], 0), preferred_element_type=jnp.float32
        )
        return tall[:SUB] + tall[SUB:]

    def solve(tiles, plan):
        first = right_mul(jnp.concatenate(tiles, 0), plan[0])
        mid = []
        for t in range(TIERS):
            spectral = left_mul(first[t * SUB : (t + 1) * SUB], plan[1])
            mid.append(left_mul(spectral * inv_den[t], plan[2]))
        last = right_mul(jnp.concatenate(mid, 0), plan[3])
        return [last[t * SUB : (t + 1) * SUB] for t in range(TIERS)]

    def start_halo(number, tiles):
        west = jnp.zeros((SUB, SUB), jnp.float32)
        east = jnp.zeros((SUB, SUB), jnp.float32)
        for k, tile in enumerate(tiles):
            row_send[number, 0, k : k + 1, :] = tile[0:1]
            row_send[number, 1, k : k + 1, :] = tile[SUB - 1 : SUB]
            west = jnp.where(full_lane == k, pltpu.roll(tile, k, 1) if k else tile, west)
            east = jnp.where(full_lane == k, pltpu.roll(tile, k + 1, 1), east)
        col_send[number, 0] = west
        col_send[number, 1] = east
        return (
            (message(col_send.at[number, 0], col_recv.at[number, 1], (i, before), not_first_col), not_last_col),
            (message(col_send.at[number, 1], col_recv.at[number, 0], (i, after), not_last_col), not_first_col),
            (message(row_send.at[number, 0], row_recv.at[number, 1], (up, j), not_first_row), not_last_row),
            (message(row_send.at[number, 1], row_recv.at[number, 0], (down, j), not_last_row), not_first_row),
        )

    def neighbours(number, k, tile):
        north = jnp.where(full_row == 0, row_recv[number, 0, k : k + 1, :], pltpu.roll(tile, 1, 0))
        south = jnp.where(
            full_row == SUB - 1, row_recv[number, 1, k : k + 1, :], pltpu.roll(tile, SUB - 1, 0)
        )
        from_west = col_recv[number, 0]
        if k:
            from_west = pltpu.roll(from_west, SUB - k, 1)
        from_east = pltpu.roll(col_recv[number, 1], SUB - 1 - k, 1)
        west = jnp.where(full_lane == 0, from_west, pltpu.roll(tile, 1, 1))
        east = jnp.where(full_lane == SUB - 1, from_east, pltpu.roll(tile, SUB - 1, 1))
        return north, south, west, east

    def gather_start(number, parts):
        total = jnp.sum(jnp.concatenate(parts, 0), axis=1, keepdims=True)
        gather_cols[number, j] = jnp.broadcast_to(total, (8, SUB))
        return [
            message(
                gather_cols.at[number, j], gather_cols.at[number, j],
                (i, lax.rem(j + step, cols)), None,
            )
            for step in range(1, cols)
        ]

    def gather_middle(number, copies):
        for copy in copies:
            receive(copy, None)
        merged = jnp.zeros((8, SUB), jnp.float32)
        for c in range(cols):
            merged = jnp.where(tile_lane == c, gather_cols[number, c], merged)
        gather_rows[number, i] = merged
        return [
            message(
                gather_rows.at[number, i], gather_rows.at[number, i],
                (lax.rem(i + step, rows), j), None,
            )
            for step in range(1, rows)
        ]

    def gather_end(number, copies):
        for copy in copies:
            receive(copy, None)
        return [gather_rows[number, r] for r in range(rows)]

    conds = []
    for t in range(TIERS):
        table = tier_table[t]
        ids = material[t]
        cond = jnp.zeros((SUB, SUB), jnp.float32)
        mean = 0.0
        mats = cond_table.shape[1]
        for m in range(mats):
            entry = cond_table[table, m]
            mean = mean + entry
            cond = jnp.where(ids == m, entry, cond)
        conds.append(cond)
        inv_mean = 1.0 / (jnp.full((8, SUB), mean, jnp.float32) * (1.0 / mats))
        inv_den[t] = recip[...] * inv_mean[0:1]

    for q in range(3):
        for route, receiver in ((fwd_route, fwd_recv), (back_route, back_recv)):

            @pl.when(jnp.logical_not(route[q][2]))
            def _():
                for apply in range(ITERS + 1):
                    for v in range(variants):
                        receiver[apply, v, q] = jnp.zeros(receiver.shape[3:], jnp.float32)

    for side, has_row, has_col in ((0, not_first_row, not_first_col), (1, not_last_row, not_last_col)):

        @pl.when(jnp.logical_not(has_row))
        def _():
            for number in range(ITERS + 1):
                row_recv[number, side] = jnp.zeros((8, SUB), jnp.float32)

        @pl.when(jnp.logical_not(has_col))
        def _():
            for number in range(ITERS + 1):
                col_recv[number, side] = jnp.zeros((SUB, SUB), jnp.float32)

    pl.semaphore_wait(
        barrier,
        cols - 1 + rows - 1 + to_front.astype(jnp.int32) + to_back.astype(jnp.int32),
    )

    def tile_sum(values):
        return jnp.sum(values, axis=0, keepdims=True)

    def start_apply(apply, get):
        return [
            send_quads(get(v), fwd_send, fwd_recv, fwd_route, apply, v) for v in range(variants)
        ]

    def residual_of(v):
        return [res[v, t] for t in range(TIERS)]

    res[...] = power[...]
    forward = start_apply(0, residual_of)
    cond_halo = start_halo(0, conds)
    zero_row = jnp.zeros((1, SUB), jnp.float32)
    sums = [
        tile_sum(sum(residual_of(v)[1:], residual_of(v)[0])) * scale for v in range(variants)
    ]
    gather = gather_start(0, [zero_row] * 6 + sums)

    mine = slots[i * cols + j]
    my_owner, my_place = lax.div(mine, own), lax.rem(mine, own)
    weights = []
    row_lane = lax.broadcasted_iota(jnp.int32, (1, SUB), 1)
    for r in range(rows):
        line = zero_row
        for c in range(cols):
            other = slots[r * cols + c]
            entry = inverse[my_owner, my_place, lax.rem(other, own)]
            entry = jnp.where(lax.div(other, own) == my_owner, entry, 0.0)
            line = jnp.where(row_lane == c, entry, line)
        weights.append(line)

    gather = gather_middle(0, gather)

    def aligned(v):
        for t, tile in enumerate(solve(residual_of(v), (0, 0, 0, 0))):
            pre[v, t] = tile

    def coarse_of(coarse_state):
        mixed = weights[0] * coarse_state[0]
        for r in range(1, rows):
            mixed = mixed + weights[r] * coarse_state[r]
        return jnp.sum(mixed, axis=1, keepdims=True) * scale

    def finish_apply(apply, forward, get_coarse):
        for v in range(variants):
            aligned(v)
        backs = []
        for v in range(variants):
            for copy, may_receive in forward[v]:
                receive(copy, may_receive)
            frames = []
            for t in range(TIERS):
                top, low_left = quad_halves(fwd_recv, apply, v, t)
                low = jnp.where(is_left, low_left, res[v, t, HALF:, :])
                frames.append(jnp.concatenate([top, low], 0))
            solved = solve(frames, (1, 2, 1, 2))
            backs.append(send_quads(solved, back_send, back_recv, back_route, apply, v))
            for t in range(TIERS):
                keep = jnp.where(is_left, 0.0, solved[t][HALF:])
                pre[v, t, HALF:, :] = pre[v, t, HALF:, :] + keep
        coarse = get_coarse()
        for v in range(variants):
            shift = coarse[6 + v : 7 + v]
            for copy, may_receive in backs[v]:
                receive(copy, may_receive)
            for t in range(TIERS):
                top, low_left = quad_halves(back_recv, apply, v, t)
                pre[v, t, :HALF, :] = pre[v, t, :HALF, :] + top + shift
                low = jnp.where(is_left, low_left, 0.0)
                pre[v, t, HALF:, :] = pre[v, t, HALF:, :] + low + shift

    for copy, may_receive in cond_halo:
        receive(copy, may_receive)
    for t in range(TIERS):
        for side, other in enumerate(neighbours(0, t, conds[t])):
            coef[t, side] = 0.5 * (conds[t] + other)
        if t + 1 < TIERS:
            upward[t] = VERT_C * 0.5 * (conds[t] + conds[t + 1])
    sink[...] = SINK_C * conds[0]

    coarse_state = None

    def first_coarse():
        nonlocal coarse_state
        coarse_state = gather_end(0, gather)
        return coarse_of(coarse_state)

    finish_apply(0, forward, first_coarse)

    rz_old = curvature = coarse_image = None
    for number in range(ITERS):
        tiles = [[pre[v, t] for t in range(TIERS)] for v in range(variants)]
        halo = start_halo(number + 1, [tile for group in tiles for tile in group])
        for copy, may_receive in halo:
            receive(copy, may_receive)
        rz_parts, uw_parts, us_parts, q_parts = [], [], [], []
        for v in range(variants):
            rz_sum = uw_sum = us_sum = q_sum = zero_row
            for t in range(TIERS):
                tile = pre[v, t]
                out = None
                for side, other in enumerate(neighbours(number + 1, v * TIERS + t, tile)):
                    term = coef[t, side] * (tile - other)
                    out = term if out is None else out + term
                if t + 1 < TIERS:
                    out = out + upward[t] * (tile - pre[v, t + 1])
                if t:
                    out = out - upward[t - 1] * (pre[v, t - 1] - tile)
                else:
                    out = out + sink[...] * tile
                image[v, t] = out
                rz_sum = rz_sum + tile_sum(res[v, t] * tile)
                uw_sum = uw_sum + tile_sum(out * tile)
                q_sum = q_sum + tile_sum(out)
                if number:
                    us_sum = us_sum + tile_sum(held_image[v, t] * tile)
            rz_parts.append(rz_sum)
            uw_parts.append(uw_sum)
            us_parts.append(us_sum)
            q_parts.append(q_sum * scale)
        gather = gather_start(number + 1, rz_parts + uw_parts + us_parts + q_parts)
        gather = gather_middle(number + 1, gather)
        gathered = gather_end(number + 1, gather)
        total = gathered[0]
        for r in range(1, rows):
            total = total + gathered[r]
        total = jnp.broadcast_to(jnp.sum(total, axis=1, keepdims=True), (8, SUB))
        rz, uw, us = total[0:2], total[2:4], total[4:6]
        if number:
            beta = rz / rz_old
            curvature = uw + 2.0 * beta * us + beta * beta * curvature
        else:
            beta = None
            curvature = uw
        alpha = rz / curvature
        rz_old = rz

        last = []
        for v in range(variants):
            step = alpha[v : v + 1]
            residuals = []
            for t in range(TIERS):
                if number:
                    turn = beta[v : v + 1]
                    moved = image[v, t] + turn * held_image[v, t]
                else:
                    moved = image[v, t]
                if number + 1 < ITERS:
                    held_image[v, t] = moved
                updated = res[v, t] - step * moved
                res[v, t] = updated
                residuals.append(updated)
            last.append(
                send_quads(residuals, fwd_send, fwd_recv, fwd_route, number + 1, v)
            )
        for v in range(variants):
            step = alpha[v : v + 1]
            for t in range(TIERS):
                if number:
                    heading = pre[v, t] + beta[v : v + 1] * held[v, t]
                    sol[v, t] = sol[v, t] + step * heading
                else:
                    heading = pre[v, t]
                    sol[v, t] = step * heading
                if number + 1 < ITERS:
                    held[v, t] = heading

        wide_alpha = jnp.concatenate([alpha] * 4, 0)
        if number:
            wide_beta = jnp.concatenate([beta] * 4, 0)
            coarse_image = [g + wide_beta * c for g, c in zip(gathered, coarse_image)]
        else:
            coarse_image = gathered
        coarse_state = [q - wide_alpha * c for q, c in zip(coarse_state, coarse_image)]
        finish_apply(number + 1, last, lambda: coarse_of(coarse_state))

    for copy, may_send in pending:
        if may_send is None:
            copy.wait_send()
        else:
            pl.when(may_send)(lambda copy=copy: copy.wait_send())


def solution(mesh):
    rows, cols = mesh.shape["rows"], mesh.shape["cols"]
    rights, lefts, recip = split_constants()

    def shards(power, material, cond_table, tier_table, coarse_slot, coarse_inverse):
        variants = power.shape[0]
        owners, own = coarse_inverse.shape[:2]
        applies = ITERS + 1
        messages = applies * variants * 6 + applies * 4 + applies * (rows - 1 + cols - 1)
        vmem = pl.BlockSpec(memory_space=pltpu.VMEM)
        smem = pl.BlockSpec(memory_space=pltpu.SMEM)
        field = (variants, TIERS, SUB, SUB)
        quad = (applies, variants, 3, TIERS // 2, HALF, SUB)

        def body(*refs):
            kernel(rows, cols, variants, owners, own, *refs)

        f32 = jnp.float32
        return pl.pallas_call(
            body,
            out_shape=[jax.ShapeDtypeStruct(power.shape, f32)] * 3,
            in_specs=[vmem] * 5 + [smem] * 4,
            out_specs=[vmem] * 3,
            scratch_shapes=[
                pltpu.VMEM((TIERS, SUB, SUB), f32),
                pltpu.VMEM((TIERS, 4, SUB, SUB), f32),
                pltpu.VMEM((TIERS - 1, SUB, SUB), f32),
                pltpu.VMEM((SUB, SUB), f32),
                pltpu.VMEM(field, f32),
                pltpu.VMEM(field, f32),
                pltpu.VMEM(field, f32),
                pltpu.VMEM(quad, f32),
                pltpu.VMEM(quad, f32),
                pltpu.VMEM(quad, f32),
                pltpu.VMEM(quad, f32),
                pltpu.VMEM((applies, 2, 8, SUB), f32),
                pltpu.VMEM((applies, 2, 8, SUB), f32),
                pltpu.VMEM((applies, 2, SUB, SUB), f32),
                pltpu.VMEM((applies, 2, SUB, SUB), f32),
                pltpu.VMEM((applies, cols, 8, SUB), f32),
                pltpu.VMEM((applies, rows, 8, SUB), f32),
                pltpu.SemaphoreType.DMA((messages,)),
                pltpu.SemaphoreType.DMA((messages,)),
            ],
            compiler_params=pltpu.CompilerParams(
                collective_id=0, has_side_effects=True, vmem_limit_bytes=48 * 1024 * 1024
            ),
        )(
            power, material, jnp.asarray(rights), jnp.asarray(lefts), jnp.asarray(recip),
            cond_table, tier_table, coarse_slot, coarse_inverse,
        )

    in_specs = (P(None, None, "rows", "cols"), P(None, "rows", "cols"), P(), P(), P(), P())
    out_specs = (P(None, None, "rows", "cols"),) * 3
    return jax.shard_map(shards, mesh=mesh, in_specs=in_specs, out_specs=out_specs, check_vma=False)
```

```python
import math

import jax
import jax.numpy as jnp
import numpy as np
from jax import lax
from jax.experimental import pallas as pl
from jax.experimental.pallas import tpu as pltpu
from jax.sharding import PartitionSpec as P

SUB = 128
HALF = SUB // 2
TIERS = 4
ITERS = 2

SHIFT_C = 0.5
VERT_C = 2.0
SINK_C = 0.05
MESH = pl.DeviceIdType.MESH


def split_constants():
    counting = np.arange(1, SUB + 1)
    angle = np.pi / (SUB + 1)
    product = (counting[:, None] * counting[None, :]) % (2 * (SUB + 1))
    basis = np.sqrt(2.0 / (SUB + 1)) * np.sin(angle * product)
    eigen = 2.0 - 2.0 * np.cos(angle * counting)
    recip = 1.0 / (eigen[:, None] + eigen[None, :] + SHIFT_C)
    rolled = np.roll(basis, HALF, axis=0)
    rights, lefts = [], []
    for matrix in (basis, rolled, rolled.T):
        high = matrix.astype(np.float32).astype(jnp.bfloat16)
        low = (matrix - high.astype(np.float64)).astype(np.float32).astype(jnp.bfloat16)
        wide = np.concatenate([high, low], 1)
        rights.append(np.concatenate([wide, wide], 0))
        tall = np.concatenate([high, low], 0)
        lefts.append(np.concatenate([tall, tall], 1))
    return np.stack(rights), np.stack(lefts), recip.astype(np.float32)


def halves(value):
    high = value.astype(jnp.bfloat16)
    low = (value - high.astype(jnp.float32)).astype(jnp.bfloat16)
    return high, low


def kernel(
    rows, cols, variants, owners, own,
    power_hbm, material_hbm, rights_hbm, lefts_hbm, recip_hbm, inverse_hbm,
    cond_table, tier_table, slots,
    sol_hbm, res_hbm, pre_hbm,
    sol, res, pre, material, rights, lefts, recip, inverse, frame_res, frame_image,
    inv_den, coef, upward, sink, held, image, held_image,
    fwd_send, fwd_recv, back_send, back_recv,
    row_send, row_recv, col_send, col_recv, gather_cols, gather_rows,
    send_sem, recv_sem, load_sem,
):
    loads = [
        pltpu.make_async_copy(source, target, load_sem.at[number])
        for number, (source, target) in enumerate((
            (material_hbm, material), (power_hbm, res), (recip_hbm, recip),
            (rights_hbm, rights), (lefts_hbm, lefts), (inverse_hbm, inverse),
        ))
    ]
    for load in loads:
        load.start()
    i, j = lax.axis_index("rows"), lax.axis_index("cols")
    not_first_row, not_last_row = i > 0, i < rows - 1
    not_first_col, not_last_col = j > 0, j < cols - 1
    up, down = jnp.maximum(i - 1, 0), jnp.minimum(i + 1, rows - 1)
    before, after = jnp.maximum(j - 1, 0), jnp.minimum(j + 1, cols - 1)
    scale = 1.0 / math.sqrt(SUB * SUB * TIERS)

    barrier = pltpu.get_barrier_semaphore()
    for step in range(1, cols):
        pl.semaphore_signal(
            barrier, 1, device_id=(i, lax.rem(j + step, cols)), device_id_type=MESH
        )
    for step in range(1, rows):
        pl.semaphore_signal(
            barrier, 1, device_id=(lax.rem(i + step, rows), j), device_id_type=MESH
        )
    to_front = jnp.logical_and(not_first_row, not_first_col)
    to_back = jnp.logical_and(not_last_row, not_last_col)

    @pl.when(to_front)
    def _():
        pl.semaphore_signal(barrier, 1, device_id=(up, before), device_id_type=MESH)

    @pl.when(to_back)
    def _():
        pl.semaphore_signal(barrier, 1, device_id=(down, after), device_id_type=MESH)

    fwd_route = (
        ((up, before), to_front, to_back),
        ((up, j), not_first_row, not_last_row),
        ((i, before), not_first_col, not_last_col),
    )
    back_route = (
        ((down, after), to_back, to_front),
        ((down, j), not_last_row, not_first_row),
        ((i, after), not_last_col, not_first_col),
    )
    quads = ((0, 0), (0, 1), (1, 0))
    counter = [0]
    pending = []

    def message(source, target, device, may_send):
        number = counter[0]
        counter[0] += 1
        copy = pltpu.make_async_remote_copy(
            source, target, send_sem.at[number], recv_sem.at[number],
            device_id=device, device_id_type=MESH,
        )
        if may_send is None:
            copy.start()
        else:
            pl.when(may_send)(lambda: copy.start())
        pending.append((copy, may_send))
        return copy

    def receive(copy, may_receive):
        if may_receive is None:
            copy.wait_recv()
        else:
            pl.when(may_receive)(lambda: copy.wait_recv())

    lane = lax.broadcasted_iota(jnp.int32, (HALF, SUB), 1)
    is_left = lane < HALF
    full_lane = lax.broadcasted_iota(jnp.int32, (SUB, SUB), 1)
    full_row = lax.broadcasted_iota(jnp.int32, (SUB, SUB), 0)
    tile_lane = lax.broadcasted_iota(jnp.int32, (8, SUB), 1)

    def swap(value):
        return pltpu.roll(value, HALF, 1)

    def send_quads(tiles, sender, receiver, route, apply, v):
        copies = []
        for q, (low, right) in enumerate(quads):
            span = slice(low * HALF, (low + 1) * HALF)
            for pair in range(TIERS // 2):
                first, second = tiles[pair][span], tiles[pair + TIERS // 2][span]
                if right:
                    packed = jnp.where(is_left, swap(first), second)
                else:
                    packed = jnp.where(is_left, first, swap(second))
                sender[apply, v, q, pair] = packed
            device, may_send, may_receive = route[q]
            copy = message(
                sender.at[apply, v, q], receiver.at[apply, v, q], device, may_send
            )
            copies.append((copy, may_receive))
        return copies

    def quad_halves(receiver, apply, v, t):
        pair, second = t % (TIERS // 2), t >= TIERS // 2
        top_left = receiver[apply, v, 0, pair]
        top_right = receiver[apply, v, 1, pair]
        low_left = receiver[apply, v, 2, pair]
        if second:
            top_left, low_left = swap(top_left), swap(low_left)
        else:
            top_right = swap(top_right)
        return jnp.where(is_left, top_left, top_right), low_left

    def right_mul(value, which):
        high, low = halves(value)
        wide = jnp.dot(
            jnp.concatenate([high, low], 1), rights[which], preferred_element_type=jnp.float32
        )
        return wide[:, :SUB] + wide[:, SUB:]

    def left_mul(value, which):
        high, low = halves(value)
        tall = jnp.dot(
            lefts[which], jnp.concatenate([high, low], 0), preferred_element_type=jnp.float32
        )
        return tall[:SUB] + tall[SUB:]

    def solve(tiles, plan):
        first = right_mul(jnp.concatenate(tiles, 0), plan[0])
        mid = []
        for t in range(TIERS):
            spectral = left_mul(first[t * SUB : (t + 1) * SUB], plan[1])
            mid.append(left_mul(spectral * inv_den[t], plan[2]))
        last = right_mul(jnp.concatenate(mid, 0), plan[3])
        return [last[t * SUB : (t + 1) * SUB] for t in range(TIERS)]

    def start_halo(number, tiles):
        west = jnp.zeros((SUB, SUB), jnp.float32)
        east = jnp.zeros((SUB, SUB), jnp.float32)
        for k, tile in enumerate(tiles):
            row_send[number, 0, k : k + 1, :] = tile[0:1]
            row_send[number, 1, k : k + 1, :] = tile[SUB - 1 : SUB]
            west = jnp.where(full_lane == k, pltpu.roll(tile, k, 1) if k else tile, west)
            east = jnp.where(full_lane == k, pltpu.roll(tile, k + 1, 1), east)
        col_send[number, 0] = west
        col_send[number, 1] = east
        return (
            (message(col_send.at[number, 0], col_recv.at[number, 1], (i, before), not_first_col), not_last_col),
            (message(col_send.at[number, 1], col_recv.at[number, 0], (i, after), not_last_col), not_first_col),
            (message(row_send.at[number, 0], row_recv.at[number, 1], (up, j), not_first_row), not_last_row),
            (message(row_send.at[number, 1], row_recv.at[number, 0], (down, j), not_last_row), not_first_row),
        )

    def neighbours(number, k, tile):
        north = jnp.where(full_row == 0, row_recv[number, 0, k : k + 1, :], pltpu.roll(tile, 1, 0))
        south = jnp.where(
            full_row == SUB - 1, row_recv[number, 1, k : k + 1, :], pltpu.roll(tile, SUB - 1, 0)
        )
        from_west = col_recv[number, 0]
        if k:
            from_west = pltpu.roll(from_west, SUB - k, 1)
        from_east = pltpu.roll(col_recv[number, 1], SUB - 1 - k, 1)
        west = jnp.where(full_lane == 0, from_west, pltpu.roll(tile, 1, 1))
        east = jnp.where(full_lane == SUB - 1, from_east, pltpu.roll(tile, SUB - 1, 1))
        return north, south, west, east

    def gather_start(number, parts):
        total = jnp.sum(jnp.concatenate(parts, 0), axis=1, keepdims=True)
        gather_cols[number, j] = jnp.broadcast_to(total, (8, SUB))
        return [
            message(
                gather_cols.at[number, j], gather_cols.at[number, j],
                (i, lax.rem(j + step, cols)), None,
            )
            for step in range(1, cols)
        ]

    def gather_middle(number, copies):
        for copy in copies:
            receive(copy, None)
        merged = jnp.zeros((8, SUB), jnp.float32)
        for c in range(cols):
            merged = jnp.where(tile_lane == c, gather_cols[number, c], merged)
        gather_rows[number, i] = merged
        return [
            message(
                gather_rows.at[number, i], gather_rows.at[number, i],
                (lax.rem(i + step, rows), j), None,
            )
            for step in range(1, rows)
        ]

    def gather_end(number, copies):
        for copy in copies:
            receive(copy, None)
        return [gather_rows[number, r] for r in range(rows)]

    for load in loads[:3]:
        load.wait()

    conds = []
    for t in range(TIERS):
        table = tier_table[t]
        ids = material[t]
        cond = jnp.zeros((SUB, SUB), jnp.float32)
        mean = 0.0
        mats = cond_table.shape[1]
        for m in range(mats):
            entry = cond_table[table, m]
            mean = mean + entry
            cond = jnp.where(ids == m, entry, cond)
        conds.append(cond)
        inv_mean = 1.0 / (jnp.full((8, SUB), mean, jnp.float32) * (1.0 / mats))
        inv_den[t] = recip[...] * inv_mean[0:1]

    for q in range(3):
        for route, receiver in ((fwd_route, fwd_recv), (back_route, back_recv)):

            @pl.when(jnp.logical_not(route[q][2]))
            def _():
                for apply in range(ITERS + 1):
                    for v in range(variants):
                        receiver[apply, v, q] = jnp.zeros(receiver.shape[3:], jnp.float32)

    for side, has_row, has_col in ((0, not_first_row, not_first_col), (1, not_last_row, not_last_col)):

        @pl.when(jnp.logical_not(has_row))
        def _():
            for number in range(ITERS * variants + 1):
                row_recv[number, side] = jnp.zeros((8, SUB), jnp.float32)

        @pl.when(jnp.logical_not(has_col))
        def _():
            for number in range(ITERS * variants + 1):
                col_recv[number, side] = jnp.zeros((SUB, SUB), jnp.float32)

    pl.semaphore_wait(
        barrier,
        cols - 1 + rows - 1 + to_front.astype(jnp.int32) + to_back.astype(jnp.int32),
    )

    def tile_sum(values):
        return jnp.sum(values, axis=0, keepdims=True)

    def start_apply(apply, get):
        return [
            send_quads(get(v), fwd_send, fwd_recv, fwd_route, apply, v) for v in range(variants)
        ]

    def residual_of(v):
        return [res[v, t] for t in range(TIERS)]

    forward = start_apply(0, residual_of)
    cond_halo = start_halo(0, conds)
    zero_row = jnp.zeros((1, SUB), jnp.float32)
    sums = [
        tile_sum(sum(residual_of(v)[1:], residual_of(v)[0])) * scale for v in range(variants)
    ]
    gather = gather_start(0, [zero_row] * 6 + sums)

    for load in loads[3:]:
        load.wait()
    mine = slots[i * cols + j]
    my_owner, my_place = lax.div(mine, own), lax.rem(mine, own)
    block = inverse[my_place]
    owner_lane = lax.broadcasted_iota(jnp.int32, block.shape, 1)
    entries = jnp.sum(jnp.where(owner_lane == my_owner, block, 0.0), axis=1, keepdims=True)
    weights = []
    row_lane = lax.broadcasted_iota(jnp.int32, (1, SUB), 1)
    for r in range(rows):
        places = jnp.full((1, SUB), -1, jnp.int32)
        for c in range(cols):
            places = jnp.where(row_lane == c, slots[r * cols + c] - my_owner * own, places)
        line = zero_row
        for k in range(own):
            line = jnp.where(places == k, entries[k : k + 1], line)
        weights.append(line)

    gather = gather_middle(0, gather)

    def coarse_of(coarse_state):
        mixed = weights[0] * coarse_state[0]
        for r in range(1, rows):
            mixed = mixed + weights[r] * coarse_state[r]
        return jnp.sum(mixed, axis=1, keepdims=True) * scale

    def solve_frames(apply, forward, own_low, update):
        backs = []
        for v in range(variants):
            for copy, may_receive in forward[v]:
                receive(copy, may_receive)
            frames = []
            for t in range(TIERS):
                top, low_left = quad_halves(fwd_recv, apply, v, t)
                low = jnp.where(is_left, low_left, own_low[v, t, HALF:, :])
                frames.append(update(v, t, jnp.concatenate([top, low], 0)))
            solved = solve(frames, (1, 2, 1, 2))
            backs.append(send_quads(solved, back_send, back_recv, back_route, apply, v))
            for t in range(TIERS):
                pre[v, t, HALF:, :] = jnp.where(is_left, 0.0, solved[t][HALF:])
        return backs

    def add_aligned(v, coarse):
        shift = coarse[6 + v : 7 + v]
        for t, tile in enumerate(solve(residual_of(v), (0, 0, 0, 0))):
            pre[v, t, :HALF, :] = tile[:HALF] + shift
            pre[v, t, HALF:, :] = pre[v, t, HALF:, :] + tile[HALF:] + shift

    def add_offset(apply, backs, v):
        for copy, may_receive in backs[v]:
            receive(copy, may_receive)
        for t in range(TIERS):
            top, low_left = quad_halves(back_recv, apply, v, t)
            pre[v, t, :HALF, :] = pre[v, t, :HALF, :] + top
            low = jnp.where(is_left, low_left, 0.0)
            pre[v, t, HALF:, :] = pre[v, t, HALF:, :] + low

    def halo_of(number, v):
        return 1 + number * variants + v

    def finish_apply(apply, backs, coarse):
        halos = []
        for v in range(variants):
            add_aligned(v, coarse)
        for v in range(variants):
            add_offset(apply, backs, v)
            if apply < ITERS:
                halos.append(start_halo(halo_of(apply, v), [pre[v, t] for t in range(TIERS)]))
            else:
                store = pltpu.make_async_copy(
                    pre.at[v], pre_hbm.at[v], load_sem.at[len(loads) + 2 + v]
                )
                store.start()
                halos.append(store)
        return halos

    for copy, may_receive in cond_halo:
        receive(copy, may_receive)
    for t in range(TIERS):
        for side, other in enumerate(neighbours(0, t, conds[t])):
            coef[t, side] = 0.5 * (conds[t] + other)
        if t + 1 < TIERS:
            upward[t] = VERT_C * 0.5 * (conds[t] + conds[t + 1])
    sink[...] = SINK_C * conds[0]

    def keep_frame(v, t, frame):
        frame_res[v, t] = frame
        return frame

    backs = solve_frames(0, forward, res, keep_frame)
    coarse_state = gather_end(0, gather)
    halos = finish_apply(0, backs, coarse_of(coarse_state))

    rz_old = curvature = coarse_image = None
    for number in range(ITERS):
        rz_parts, uw_parts, us_parts, q_parts, forward = [], [], [], [], []

        def apply_operator(v):
            for copy, may_receive in halos[v]:
                receive(copy, may_receive)
            rz_sum = uw_sum = us_sum = q_sum = zero_row
            for t in range(TIERS):
                tile = pre[v, t]
                out = None
                for side, other in enumerate(neighbours(halo_of(number, v), t, tile)):
                    term = coef[t, side] * (tile - other)
                    out = term if out is None else out + term
                if t + 1 < TIERS:
                    out = out + upward[t] * (tile - pre[v, t + 1])
                if t:
                    out = out - upward[t - 1] * (pre[v, t - 1] - tile)
                else:
                    out = out + sink[...] * tile
                image[v, t] = out
                rz_sum = rz_sum + tile_sum(res[v, t] * tile)
                uw_sum = uw_sum + tile_sum(out * tile)
                q_sum = q_sum + tile_sum(out)
                if number:
                    us_sum = us_sum + tile_sum(held_image[v, t] * tile)
            rz_parts.append(rz_sum)
            uw_parts.append(uw_sum)
            us_parts.append(us_sum)
            q_parts.append(q_sum * scale)

        def send_image(v):
            forward.append(
                send_quads(
                    [image[v, t] for t in range(TIERS)],
                    fwd_send, fwd_recv, fwd_route, number + 1, v,
                )
            )

        for v in range(variants):
            if v:
                send_image(v - 1)
            apply_operator(v)
        gather = gather_start(number + 1, rz_parts + uw_parts + us_parts + q_parts)
        send_image(variants - 1)
        gather = gather_middle(number + 1, gather)
        gathered = gather_end(number + 1, gather)
        total = gathered[0]
        for r in range(1, rows):
            total = total + gathered[r]
        total = jnp.broadcast_to(jnp.sum(total, axis=1, keepdims=True), (8, SUB))
        rz, uw, us = total[0:2], total[2:4], total[4:6]
        if number:
            beta = rz / rz_old
            curvature = uw + 2.0 * beta * us + beta * beta * curvature
        else:
            beta = None
            curvature = uw
        alpha = rz / curvature
        rz_old = rz

        def update_frame(v, t, frame):
            if number:
                frame = frame + beta[v : v + 1] * frame_image[v, t]
            if number + 1 < ITERS:
                frame_image[v, t] = frame
            updated = frame_res[v, t] - alpha[v : v + 1] * frame
            if number + 1 < ITERS:
                frame_res[v, t] = updated
            return updated

        for v in range(variants):
            step = alpha[v : v + 1]
            for t in range(TIERS):
                if number:
                    heading = pre[v, t] + beta[v : v + 1] * held[v, t]
                    sol[v, t] = sol[v, t] + step * heading
                else:
                    heading = pre[v, t]
                    sol[v, t] = step * heading
                if number + 1 < ITERS:
                    held[v, t] = heading
        backs = solve_frames(number + 1, forward, image, update_frame)
        for v in range(variants):
            step = alpha[v : v + 1]
            for t in range(TIERS):
                moved = image[v, t]
                if number:
                    moved = moved + beta[v : v + 1] * held_image[v, t]
                if number + 1 < ITERS:
                    held_image[v, t] = moved
                res[v, t] = res[v, t] - step * moved

        wide_alpha = jnp.concatenate([alpha] * 4, 0)
        if number:
            wide_beta = jnp.concatenate([beta] * 4, 0)
            coarse_image = [g + wide_beta * c for g, c in zip(gathered, coarse_image)]
        else:
            coarse_image = gathered
        coarse_state = [q - wide_alpha * c for q, c in zip(coarse_state, coarse_image)]
        if number + 1 == ITERS:
            stores = [
                pltpu.make_async_copy(sol, sol_hbm, load_sem.at[len(loads)]),
                pltpu.make_async_copy(res, res_hbm, load_sem.at[len(loads) + 1]),
            ]
            for store in stores:
                store.start()
        halos = finish_apply(number + 1, backs, coarse_of(coarse_state))

    for store in stores + halos:
        store.wait()
    for copy, may_send in pending:
        if may_send is None:
            copy.wait_send()
        else:
            pl.when(may_send)(lambda copy=copy: copy.wait_send())


def write_out(*refs):
    count = len(refs) // 2
    sources, targets, sem = refs[:count], refs[count : 2 * count], refs[-1]
    copies = [
        pltpu.make_async_copy(source, target, sem.at[number])
        for number, (source, target) in enumerate(zip(sources, targets))
    ]
    for copy in copies:
        copy.start()
    for copy in copies:
        copy.wait()


def solution(mesh):
    rows, cols = mesh.shape["rows"], mesh.shape["cols"]
    rights, lefts, recip = split_constants()

    def shards(power, material, cond_table, tier_table, coarse_slot, coarse_inverse):
        variants = power.shape[0]
        owners, own = coarse_inverse.shape[:2]
        applies = ITERS + 1
        halos = ITERS * variants + 1
        messages = applies * variants * 6 + halos * 4 + applies * (rows - 1 + cols - 1)
        hbm = pl.BlockSpec(memory_space=pltpu.HBM)
        smem = pl.BlockSpec(memory_space=pltpu.SMEM)
        field = (variants, TIERS, SUB, SUB)
        quad = (applies, variants, 3, TIERS // 2, HALF, SUB)

        def body(*refs):
            kernel(rows, cols, variants, owners, own, *refs)

        f32 = jnp.float32
        done = pl.pallas_call(
            body,
            out_shape=[jax.ShapeDtypeStruct(power.shape, f32)] * 3,
            in_specs=[hbm] * 6 + [smem] * 3,
            out_specs=[hbm] * 3,
            scratch_shapes=[
                pltpu.VMEM(field, f32),
                pltpu.VMEM(field, f32),
                pltpu.VMEM(field, f32),
                pltpu.VMEM((TIERS, SUB, SUB), jnp.int32),
                pltpu.VMEM(rights.shape, jnp.bfloat16),
                pltpu.VMEM(lefts.shape, jnp.bfloat16),
                pltpu.VMEM((SUB, SUB), f32),
                pltpu.VMEM((own, own, owners), f32),
                pltpu.VMEM(field, f32),
                pltpu.VMEM(field, f32),
                pltpu.VMEM((TIERS, SUB, SUB), f32),
                pltpu.VMEM((TIERS, 4, SUB, SUB), f32),
                pltpu.VMEM((TIERS - 1, SUB, SUB), f32),
                pltpu.VMEM((SUB, SUB), f32),
                pltpu.VMEM(field, f32),
                pltpu.VMEM(field, f32),
                pltpu.VMEM(field, f32),
                pltpu.VMEM(quad, f32),
                pltpu.VMEM(quad, f32),
                pltpu.VMEM(quad, f32),
                pltpu.VMEM(quad, f32),
                pltpu.VMEM((halos, 2, 8, SUB), f32),
                pltpu.VMEM((halos, 2, 8, SUB), f32),
                pltpu.VMEM((halos, 2, SUB, SUB), f32),
                pltpu.VMEM((halos, 2, SUB, SUB), f32),
                pltpu.VMEM((applies, cols, 8, SUB), f32),
                pltpu.VMEM((applies, rows, 8, SUB), f32),
                pltpu.SemaphoreType.DMA((messages,)),
                pltpu.SemaphoreType.DMA((messages,)),
                pltpu.SemaphoreType.DMA((8 + variants,)),
            ],
            compiler_params=pltpu.CompilerParams(
                collective_id=0, has_side_effects=True, vmem_limit_bytes=60 * 1024 * 1024
            ),
        )(
            power, material, jnp.asarray(rights), jnp.asarray(lefts), jnp.asarray(recip),
            jnp.transpose(coarse_inverse, (1, 2, 0)), cond_table, tier_table, coarse_slot,
        )
        return pl.pallas_call(
            write_out,
            out_shape=[jax.ShapeDtypeStruct(power.shape, f32)] * 3,
            in_specs=[hbm] * 3,
            out_specs=[hbm] * 3,
            scratch_shapes=[pltpu.SemaphoreType.DMA((3,))],
            compiler_params=pltpu.CompilerParams(vmem_limit_bytes=60 * 1024 * 1024),
        )(*done)

    in_specs = (P(None, None, "rows", "cols"), P(None, "rows", "cols"), P(), P(), P(), P())
    out_specs = (P(None, None, "rows", "cols"),) * 3
    return jax.shard_map(shards, mesh=mesh, in_specs=in_specs, out_specs=out_specs, check_vma=False)
```

```python
import math

import jax
import jax.numpy as jnp
import numpy as np
from jax import lax
from jax.experimental import pallas as pl
from jax.experimental.pallas import tpu as pltpu
from jax.sharding import PartitionSpec as P

SUB = 128
HALF = SUB // 2
TIERS = 4
ITERS = 2

SHIFT_C = 0.5
VERT_C = 2.0
SINK_C = 0.05
MESH = pl.DeviceIdType.MESH


def split_constants():
    counting = np.arange(1, SUB + 1)
    angle = np.pi / (SUB + 1)
    product = (counting[:, None] * counting[None, :]) % (2 * (SUB + 1))
    basis = np.sqrt(2.0 / (SUB + 1)) * np.sin(angle * product)
    eigen = 2.0 - 2.0 * np.cos(angle * counting)
    recip = 1.0 / (eigen[:, None] + eigen[None, :] + SHIFT_C)
    rolled = np.roll(basis, HALF, axis=0)
    rights, lefts = [], []
    for matrix in (basis, rolled, rolled.T):
        high = matrix.astype(np.float32).astype(jnp.bfloat16)
        low = (matrix - high.astype(np.float64)).astype(np.float32).astype(jnp.bfloat16)
        wide = np.concatenate([high, low], 1)
        rights.append(np.concatenate([wide, wide], 0))
        tall = np.concatenate([high, low], 0)
        lefts.append(np.concatenate([tall, tall], 1))
    return np.stack(rights), np.stack(lefts), recip.astype(np.float32)


def halves(value):
    high = value.astype(jnp.bfloat16)
    low = (value - high.astype(jnp.float32)).astype(jnp.bfloat16)
    return high, low


def kernel(
    rows, cols, variants, owners, own,
    power_hbm, material_hbm, rights_hbm, lefts_hbm, recip_hbm, inverse_hbm,
    cond_table, tier_table, slots,
    sol, res, pre, material, rights, lefts, recip, inverse, frame_res, frame_image,
    inv_den, coef, upward, sink, held, image, held_image,
    fwd_send, fwd_recv, back_send, back_recv,
    row_send, row_recv, col_send, col_recv, gather_cols, gather_rows,
    send_sem, recv_sem, load_sem,
):
    loads = [
        pltpu.make_async_copy(source, target, load_sem.at[number])
        for number, (source, target) in enumerate((
            (material_hbm, material), (power_hbm, res), (recip_hbm, recip),
            (rights_hbm, rights), (lefts_hbm, lefts), (inverse_hbm, inverse),
        ))
    ]
    for load in loads:
        load.start()
    i, j = lax.axis_index("rows"), lax.axis_index("cols")
    not_first_row, not_last_row = i > 0, i < rows - 1
    not_first_col, not_last_col = j > 0, j < cols - 1
    up, down = jnp.maximum(i - 1, 0), jnp.minimum(i + 1, rows - 1)
    before, after = jnp.maximum(j - 1, 0), jnp.minimum(j + 1, cols - 1)
    scale = 1.0 / math.sqrt(SUB * SUB * TIERS)

    barrier = pltpu.get_barrier_semaphore()
    for step in range(1, cols):
        pl.semaphore_signal(
            barrier, 1, device_id=(i, lax.rem(j + step, cols)), device_id_type=MESH
        )
    for step in range(1, rows):
        pl.semaphore_signal(
            barrier, 1, device_id=(lax.rem(i + step, rows), j), device_id_type=MESH
        )
    to_front = jnp.logical_and(not_first_row, not_first_col)
    to_back = jnp.logical_and(not_last_row, not_last_col)

    @pl.when(to_front)
    def _():
        pl.semaphore_signal(barrier, 1, device_id=(up, before), device_id_type=MESH)

    @pl.when(to_back)
    def _():
        pl.semaphore_signal(barrier, 1, device_id=(down, after), device_id_type=MESH)

    fwd_route = (
        ((up, before), to_front, to_back),
        ((up, j), not_first_row, not_last_row),
        ((i, before), not_first_col, not_last_col),
    )
    back_route = (
        ((down, after), to_back, to_front),
        ((down, j), not_last_row, not_first_row),
        ((i, after), not_last_col, not_first_col),
    )
    quads = ((0, 0), (0, 1), (1, 0))
    counter = [0]
    pending = []

    def message(source, target, device, may_send):
        number = counter[0]
        counter[0] += 1
        copy = pltpu.make_async_remote_copy(
            source, target, send_sem.at[number], recv_sem.at[number],
            device_id=device, device_id_type=MESH,
        )
        if may_send is None:
            copy.start()
        else:
            pl.when(may_send)(lambda: copy.start())
        pending.append((copy, may_send))
        return copy

    def receive(copy, may_receive):
        if may_receive is None:
            copy.wait_recv()
        else:
            pl.when(may_receive)(lambda: copy.wait_recv())

    lane = lax.broadcasted_iota(jnp.int32, (HALF, SUB), 1)
    is_left = lane < HALF
    full_lane = lax.broadcasted_iota(jnp.int32, (SUB, SUB), 1)
    full_row = lax.broadcasted_iota(jnp.int32, (SUB, SUB), 0)
    tile_lane = lax.broadcasted_iota(jnp.int32, (8, SUB), 1)

    def swap(value):
        return pltpu.roll(value, HALF, 1)

    def send_quads(tiles, sender, receiver, route, apply, v):
        copies = []
        for q, (low, right) in enumerate(quads):
            span = slice(low * HALF, (low + 1) * HALF)
            for pair in range(TIERS // 2):
                first, second = tiles[pair][span], tiles[pair + TIERS // 2][span]
                if right:
                    packed = jnp.where(is_left, swap(first), second)
                else:
                    packed = jnp.where(is_left, first, swap(second))
                sender[apply, v, q, pair] = packed
            device, may_send, may_receive = route[q]
            copy = message(
                sender.at[apply, v, q], receiver.at[apply, v, q], device, may_send
            )
            copies.append((copy, may_receive))
        return copies

    def quad_halves(receiver, apply, v, t):
        pair, second = t % (TIERS // 2), t >= TIERS // 2
        top_left = receiver[apply, v, 0, pair]
        top_right = receiver[apply, v, 1, pair]
        low_left = receiver[apply, v, 2, pair]
        if second:
            top_left, low_left = swap(top_left), swap(low_left)
        else:
            top_right = swap(top_right)
        return jnp.where(is_left, top_left, top_right), low_left

    def right_mul(value, which):
        high, low = halves(value)
        wide = jnp.dot(
            jnp.concatenate([high, low], 1), rights[which], preferred_element_type=jnp.float32
        )
        return wide[:, :SUB] + wide[:, SUB:]

    def left_mul(value, which):
        high, low = halves(value)
        tall = jnp.dot(
            lefts[which], jnp.concatenate([high, low], 0), preferred_element_type=jnp.float32
        )
        return tall[:SUB] + tall[SUB:]

    def solve(tiles, plan):
        first = right_mul(jnp.concatenate(tiles, 0), plan[0])
        mid = []
        for t in range(TIERS):
            spectral = left_mul(first[t * SUB : (t + 1) * SUB], plan[1])
            mid.append(left_mul(spectral * inv_den[t], plan[2]))
        last = right_mul(jnp.concatenate(mid, 0), plan[3])
        return [last[t * SUB : (t + 1) * SUB] for t in range(TIERS)]

    def start_halo(number, tiles):
        west = jnp.zeros((SUB, SUB), jnp.float32)
        east = jnp.zeros((SUB, SUB), jnp.float32)
        for k, tile in enumerate(tiles):
            row_send[number, 0, k : k + 1, :] = tile[0:1]
            row_send[number, 1, k : k + 1, :] = tile[SUB - 1 : SUB]
            west = jnp.where(full_lane == k, pltpu.roll(tile, k, 1) if k else tile, west)
            east = jnp.where(full_lane == k, pltpu.roll(tile, k + 1, 1), east)
        col_send[number, 0] = west
        col_send[number, 1] = east
        return (
            (message(col_send.at[number, 0], col_recv.at[number, 1], (i, before), not_first_col), not_last_col),
            (message(col_send.at[number, 1], col_recv.at[number, 0], (i, after), not_last_col), not_first_col),
            (message(row_send.at[number, 0], row_recv.at[number, 1], (up, j), not_first_row), not_last_row),
            (message(row_send.at[number, 1], row_recv.at[number, 0], (down, j), not_last_row), not_first_row),
        )

    def neighbours(number, k, tile):
        north = jnp.where(full_row == 0, row_recv[number, 0, k : k + 1, :], pltpu.roll(tile, 1, 0))
        south = jnp.where(
            full_row == SUB - 1, row_recv[number, 1, k : k + 1, :], pltpu.roll(tile, SUB - 1, 0)
        )
        from_west = col_recv[number, 0]
        if k:
            from_west = pltpu.roll(from_west, SUB - k, 1)
        from_east = pltpu.roll(col_recv[number, 1], SUB - 1 - k, 1)
        west = jnp.where(full_lane == 0, from_west, pltpu.roll(tile, 1, 1))
        east = jnp.where(full_lane == SUB - 1, from_east, pltpu.roll(tile, SUB - 1, 1))
        return north, south, west, east

    def gather_start(number, parts):
        total = jnp.sum(jnp.concatenate(parts, 0), axis=1, keepdims=True)
        gather_cols[number, j] = jnp.broadcast_to(total, (8, SUB))
        return [
            message(
                gather_cols.at[number, j], gather_cols.at[number, j],
                (i, lax.rem(j + step, cols)), None,
            )
            for step in range(1, cols)
        ]

    def gather_middle(number, copies):
        for copy in copies:
            receive(copy, None)
        merged = jnp.zeros((8, SUB), jnp.float32)
        for c in range(cols):
            merged = jnp.where(tile_lane == c, gather_cols[number, c], merged)
        gather_rows[number, i] = merged
        return [
            message(
                gather_rows.at[number, i], gather_rows.at[number, i],
                (lax.rem(i + step, rows), j), None,
            )
            for step in range(1, rows)
        ]

    def gather_end(number, copies):
        for copy in copies:
            receive(copy, None)
        return [gather_rows[number, r] for r in range(rows)]

    for load in loads[:3]:
        load.wait()

    conds = []
    for t in range(TIERS):
        table = tier_table[t]
        ids = material[t]
        cond = jnp.zeros((SUB, SUB), jnp.float32)
        mean = 0.0
        mats = cond_table.shape[1]
        for m in range(mats):
            entry = cond_table[table, m]
            mean = mean + entry
            cond = jnp.where(ids == m, entry, cond)
        conds.append(cond)
        inv_mean = 1.0 / (jnp.full((8, SUB), mean, jnp.float32) * (1.0 / mats))
        inv_den[t] = recip[...] * inv_mean[0:1]

    for q in range(3):
        for route, receiver in ((fwd_route, fwd_recv), (back_route, back_recv)):

            @pl.when(jnp.logical_not(route[q][2]))
            def _():
                for apply in range(ITERS + 1):
                    for v in range(variants):
                        receiver[apply, v, q] = jnp.zeros(receiver.shape[3:], jnp.float32)

    for side, has_row, has_col in ((0, not_first_row, not_first_col), (1, not_last_row, not_last_col)):

        @pl.when(jnp.logical_not(has_row))
        def _():
            for number in range(ITERS * variants + 1):
                row_recv[number, side] = jnp.zeros((8, SUB), jnp.float32)

        @pl.when(jnp.logical_not(has_col))
        def _():
            for number in range(ITERS * variants + 1):
                col_recv[number, side] = jnp.zeros((SUB, SUB), jnp.float32)

    pl.semaphore_wait(
        barrier,
        cols - 1 + rows - 1 + to_front.astype(jnp.int32) + to_back.astype(jnp.int32),
    )

    def tile_sum(values):
        return jnp.sum(values, axis=0, keepdims=True)

    def start_apply(apply, get):
        return [
            send_quads(get(v), fwd_send, fwd_recv, fwd_route, apply, v) for v in range(variants)
        ]

    def residual_of(v):
        return [res[v, t] for t in range(TIERS)]

    forward = start_apply(0, residual_of)
    cond_halo = start_halo(0, conds)
    zero_row = jnp.zeros((1, SUB), jnp.float32)
    sums = [
        tile_sum(sum(residual_of(v)[1:], residual_of(v)[0])) * scale for v in range(variants)
    ]
    gather = gather_start(0, [zero_row] * 6 + sums)

    for load in loads[3:]:
        load.wait()
    mine = slots[i * cols + j]
    my_owner, my_place = lax.div(mine, own), lax.rem(mine, own)
    block = inverse[my_place]
    owner_lane = lax.broadcasted_iota(jnp.int32, block.shape, 1)
    entries = jnp.sum(jnp.where(owner_lane == my_owner, block, 0.0), axis=1, keepdims=True)
    weights = []
    row_lane = lax.broadcasted_iota(jnp.int32, (1, SUB), 1)
    for r in range(rows):
        places = jnp.full((1, SUB), -1, jnp.int32)
        for c in range(cols):
            places = jnp.where(row_lane == c, slots[r * cols + c] - my_owner * own, places)
        line = zero_row
        for k in range(own):
            line = jnp.where(places == k, entries[k : k + 1], line)
        weights.append(line)

    gather = gather_middle(0, gather)

    def coarse_of(coarse_state):
        mixed = weights[0] * coarse_state[0]
        for r in range(1, rows):
            mixed = mixed + weights[r] * coarse_state[r]
        return jnp.sum(mixed, axis=1, keepdims=True) * scale

    def solve_frames(apply, forward, own_low, update):
        backs = []
        for v in range(variants):
            for copy, may_receive in forward[v]:
                receive(copy, may_receive)
            frames = []
            for t in range(TIERS):
                top, low_left = quad_halves(fwd_recv, apply, v, t)
                low = jnp.where(is_left, low_left, own_low[v, t, HALF:, :])
                frames.append(update(v, t, jnp.concatenate([top, low], 0)))
            solved = solve(frames, (1, 2, 1, 2))
            backs.append(send_quads(solved, back_send, back_recv, back_route, apply, v))
            for t in range(TIERS):
                pre[v, t, HALF:, :] = jnp.where(is_left, 0.0, solved[t][HALF:])
        return backs

    def add_aligned(v, coarse):
        shift = coarse[6 + v : 7 + v]
        for t, tile in enumerate(solve(residual_of(v), (0, 0, 0, 0))):
            pre[v, t, :HALF, :] = tile[:HALF] + shift
            pre[v, t, HALF:, :] = pre[v, t, HALF:, :] + tile[HALF:] + shift

    def add_offset(apply, backs, v):
        for copy, may_receive in backs[v]:
            receive(copy, may_receive)
        for t in range(TIERS):
            top, low_left = quad_halves(back_recv, apply, v, t)
            pre[v, t, :HALF, :] = pre[v, t, :HALF, :] + top
            low = jnp.where(is_left, low_left, 0.0)
            pre[v, t, HALF:, :] = pre[v, t, HALF:, :] + low

    def halo_of(number, v):
        return 1 + number * variants + v

    def finish_apply(apply, backs, coarse):
        halos = []
        for v in range(variants):
            add_aligned(v, coarse)
        for v in range(variants):
            add_offset(apply, backs, v)
            if apply < ITERS:
                halos.append(start_halo(halo_of(apply, v), [pre[v, t] for t in range(TIERS)]))
        return halos

    for copy, may_receive in cond_halo:
        receive(copy, may_receive)
    for t in range(TIERS):
        for side, other in enumerate(neighbours(0, t, conds[t])):
            coef[t, side] = 0.5 * (conds[t] + other)
        if t + 1 < TIERS:
            upward[t] = VERT_C * 0.5 * (conds[t] + conds[t + 1])
    sink[...] = SINK_C * conds[0]

    def keep_frame(v, t, frame):
        frame_res[v, t] = frame
        return frame

    backs = solve_frames(0, forward, res, keep_frame)
    coarse_state = gather_end(0, gather)
    halos = finish_apply(0, backs, coarse_of(coarse_state))

    rz_old = curvature = coarse_image = None
    for number in range(ITERS):
        rz_parts, uw_parts, us_parts, q_parts, forward = [], [], [], [], []

        def apply_operator(v):
            for copy, may_receive in halos[v]:
                receive(copy, may_receive)
            rz_sum = uw_sum = us_sum = q_sum = zero_row
            for t in range(TIERS):
                tile = pre[v, t]
                out = None
                for side, other in enumerate(neighbours(halo_of(number, v), t, tile)):
                    term = coef[t, side] * (tile - other)
                    out = term if out is None else out + term
                if t + 1 < TIERS:
                    out = out + upward[t] * (tile - pre[v, t + 1])
                if t:
                    out = out - upward[t - 1] * (pre[v, t - 1] - tile)
                else:
                    out = out + sink[...] * tile
                image[v, t] = out
                rz_sum = rz_sum + tile_sum(res[v, t] * tile)
                uw_sum = uw_sum + tile_sum(out * tile)
                q_sum = q_sum + tile_sum(out)
                if number:
                    us_sum = us_sum + tile_sum(held_image[v, t] * tile)
            rz_parts.append(rz_sum)
            uw_parts.append(uw_sum)
            us_parts.append(us_sum)
            q_parts.append(q_sum * scale)

        def send_image(v):
            forward.append(
                send_quads(
                    [image[v, t] for t in range(TIERS)],
                    fwd_send, fwd_recv, fwd_route, number + 1, v,
                )
            )

        for v in range(variants):
            if v:
                send_image(v - 1)
            apply_operator(v)
        gather = gather_start(number + 1, rz_parts + uw_parts + us_parts + q_parts)
        send_image(variants - 1)
        gather = gather_middle(number + 1, gather)
        gathered = gather_end(number + 1, gather)
        total = gathered[0]
        for r in range(1, rows):
            total = total + gathered[r]
        total = jnp.broadcast_to(jnp.sum(total, axis=1, keepdims=True), (8, SUB))
        rz, uw, us = total[0:2], total[2:4], total[4:6]
        if number:
            beta = rz / rz_old
            curvature = uw + 2.0 * beta * us + beta * beta * curvature
        else:
            beta = None
            curvature = uw
        alpha = rz / curvature
        rz_old = rz

        def update_frame(v, t, frame):
            if number:
                frame = frame + beta[v : v + 1] * frame_image[v, t]
            if number + 1 < ITERS:
                frame_image[v, t] = frame
            updated = frame_res[v, t] - alpha[v : v + 1] * frame
            if number + 1 < ITERS:
                frame_res[v, t] = updated
            return updated

        for v in range(variants):
            step = alpha[v : v + 1]
            for t in range(TIERS):
                if number:
                    heading = pre[v, t] + beta[v : v + 1] * held[v, t]
                    sol[v, t] = sol[v, t] + step * heading
                else:
                    heading = pre[v, t]
                    sol[v, t] = step * heading
                if number + 1 < ITERS:
                    held[v, t] = heading
        backs = solve_frames(number + 1, forward, image, update_frame)
        for v in range(variants):
            step = alpha[v : v + 1]
            for t in range(TIERS):
                moved = image[v, t]
                if number:
                    moved = moved + beta[v : v + 1] * held_image[v, t]
                if number + 1 < ITERS:
                    held_image[v, t] = moved
                res[v, t] = res[v, t] - step * moved

        wide_alpha = jnp.concatenate([alpha] * 4, 0)
        if number:
            wide_beta = jnp.concatenate([beta] * 4, 0)
            coarse_image = [g + wide_beta * c for g, c in zip(gathered, coarse_image)]
        else:
            coarse_image = gathered
        coarse_state = [q - wide_alpha * c for q, c in zip(coarse_state, coarse_image)]
        halos = finish_apply(number + 1, backs, coarse_of(coarse_state))

    for copy, may_send in pending:
        if may_send is None:
            copy.wait_send()
        else:
            pl.when(may_send)(lambda copy=copy: copy.wait_send())


def write_out(*refs):
    count = len(refs) // 2
    sources, targets, sem = refs[:count], refs[count : 2 * count], refs[-1]
    copies = [
        pltpu.make_async_copy(source, target, sem.at[number])
        for number, (source, target) in enumerate(zip(sources, targets))
    ]
    for copy in copies:
        copy.start()
    for copy in copies:
        copy.wait()


def solution(mesh):
    rows, cols = mesh.shape["rows"], mesh.shape["cols"]
    rights, lefts, recip = split_constants()

    def shards(power, material, cond_table, tier_table, coarse_slot, coarse_inverse):
        variants = power.shape[0]
        owners, own = coarse_inverse.shape[:2]
        applies = ITERS + 1
        halos = ITERS * variants + 1
        messages = applies * variants * 6 + halos * 4 + applies * (rows - 1 + cols - 1)
        hbm = pl.BlockSpec(memory_space=pltpu.HBM)
        vmem = pl.BlockSpec(memory_space=pltpu.VMEM)
        smem = pl.BlockSpec(memory_space=pltpu.SMEM)
        field = (variants, TIERS, SUB, SUB)
        quad = (applies, variants, 3, TIERS // 2, HALF, SUB)

        def body(*refs):
            kernel(rows, cols, variants, owners, own, *refs)

        f32 = jnp.float32
        done = pl.pallas_call(
            body,
            out_shape=[pltpu.VMEM(power.shape, f32)] * 3,
            in_specs=[hbm] * 6 + [smem] * 3,
            out_specs=[vmem] * 3,
            scratch_shapes=[
                pltpu.VMEM((TIERS, SUB, SUB), jnp.int32),
                pltpu.VMEM(rights.shape, jnp.bfloat16),
                pltpu.VMEM(lefts.shape, jnp.bfloat16),
                pltpu.VMEM((SUB, SUB), f32),
                pltpu.VMEM((own, own, owners), f32),
                pltpu.VMEM(field, f32),
                pltpu.VMEM(field, f32),
                pltpu.VMEM((TIERS, SUB, SUB), f32),
                pltpu.VMEM((TIERS, 4, SUB, SUB), f32),
                pltpu.VMEM((TIERS - 1, SUB, SUB), f32),
                pltpu.VMEM((SUB, SUB), f32),
                pltpu.VMEM(field, f32),
                pltpu.VMEM(field, f32),
                pltpu.VMEM(field, f32),
                pltpu.VMEM(quad, f32),
                pltpu.VMEM(quad, f32),
                pltpu.VMEM(quad, f32),
                pltpu.VMEM(quad, f32),
                pltpu.VMEM((halos, 2, 8, SUB), f32),
                pltpu.VMEM((halos, 2, 8, SUB), f32),
                pltpu.VMEM((halos, 2, SUB, SUB), f32),
                pltpu.VMEM((halos, 2, SUB, SUB), f32),
                pltpu.VMEM((applies, cols, 8, SUB), f32),
                pltpu.VMEM((applies, rows, 8, SUB), f32),
                pltpu.SemaphoreType.DMA((messages,)),
                pltpu.SemaphoreType.DMA((messages,)),
                pltpu.SemaphoreType.DMA((6,)),
            ],
            compiler_params=pltpu.CompilerParams(
                collective_id=0, has_side_effects=True, vmem_limit_bytes=58 * 1024 * 1024
            ),
        )(
            power, material, jnp.asarray(rights), jnp.asarray(lefts), jnp.asarray(recip),
            jnp.transpose(coarse_inverse, (1, 2, 0)), cond_table, tier_table, coarse_slot,
        )
        return pl.pallas_call(
            write_out,
            out_shape=[jax.ShapeDtypeStruct(power.shape, f32)] * 3,
            in_specs=[vmem] * 3,
            out_specs=[hbm] * 3,
            scratch_shapes=[pltpu.SemaphoreType.DMA((3,))],
            compiler_params=pltpu.CompilerParams(vmem_limit_bytes=8 * 1024 * 1024),
        )(*done)

    in_specs = (P(None, None, "rows", "cols"), P(None, "rows", "cols"), P(), P(), P(), P())
    out_specs = (P(None, None, "rows", "cols"),) * 3
    return jax.shard_map(shards, mesh=mesh, in_specs=in_specs, out_specs=out_specs, check_vma=False)
```

```python
import math

import jax
import jax.numpy as jnp
import numpy as np
from jax import lax
from jax.experimental import pallas as pl
from jax.experimental.pallas import tpu as pltpu
from jax.sharding import PartitionSpec as P

SUB = 128
HALF = SUB // 2
TIERS = 4
ITERS = 2

SHIFT_C = 0.5
VERT_C = 2.0
SINK_C = 0.05
MESH = pl.DeviceIdType.MESH


def split_constants():
    counting = np.arange(1, SUB + 1)
    angle = np.pi / (SUB + 1)
    product = (counting[:, None] * counting[None, :]) % (2 * (SUB + 1))
    basis = np.sqrt(2.0 / (SUB + 1)) * np.sin(angle * product)
    eigen = 2.0 - 2.0 * np.cos(angle * counting)
    recip = 1.0 / (eigen[:, None] + eigen[None, :] + SHIFT_C)
    rolled = np.roll(basis, HALF, axis=0)
    rights, lefts = [], []
    for matrix in (basis, rolled, rolled.T):
        high = matrix.astype(np.float32).astype(jnp.bfloat16)
        low = (matrix - high.astype(np.float64)).astype(np.float32).astype(jnp.bfloat16)
        wide = np.concatenate([high, low], 1)
        rights.append(np.concatenate([wide, wide], 0))
        tall = np.concatenate([high, low], 0)
        lefts.append(np.concatenate([tall, tall], 1))
    return np.stack(rights), np.stack(lefts), recip.astype(np.float32)


def halves(value):
    high = value.astype(jnp.bfloat16)
    low = (value - high.astype(jnp.float32)).astype(jnp.bfloat16)
    return high, low


def kernel(
    rows, cols, variants, owners, own,
    power_hbm, material_hbm, rights_hbm, lefts_hbm, recip_hbm, inverse_hbm,
    cond_table, tier_table, slots,
    sol, res, pre, material, rights, lefts, recip, inverse, frame_res, frame_image,
    inv_den, coef, upward, sink, held, image, held_image,
    fwd_send, fwd_recv, back_send, back_recv,
    row_send, row_recv, col_send, col_recv, gather_cols, gather_rows,
    send_sem, recv_sem, load_sem,
):
    loads = [
        pltpu.make_async_copy(source, target, load_sem.at[number])
        for number, (source, target) in enumerate((
            (material_hbm, material), (power_hbm, res), (recip_hbm, recip),
            (rights_hbm, rights), (lefts_hbm, lefts), (inverse_hbm, inverse),
        ))
    ]
    for load in loads:
        load.start()
    i, j = lax.axis_index("rows"), lax.axis_index("cols")
    not_first_row, not_last_row = i > 0, i < rows - 1
    not_first_col, not_last_col = j > 0, j < cols - 1
    up, down = jnp.maximum(i - 1, 0), jnp.minimum(i + 1, rows - 1)
    before, after = jnp.maximum(j - 1, 0), jnp.minimum(j + 1, cols - 1)
    scale = 1.0 / math.sqrt(SUB * SUB * TIERS)

    barrier = pltpu.get_barrier_semaphore()
    for step in range(1, cols):
        pl.semaphore_signal(
            barrier, 1, device_id=(i, lax.rem(j + step, cols)), device_id_type=MESH
        )
    for step in range(1, rows):
        pl.semaphore_signal(
            barrier, 1, device_id=(lax.rem(i + step, rows), j), device_id_type=MESH
        )
    to_front = jnp.logical_and(not_first_row, not_first_col)
    to_back = jnp.logical_and(not_last_row, not_last_col)

    @pl.when(to_front)
    def _():
        pl.semaphore_signal(barrier, 1, device_id=(up, before), device_id_type=MESH)

    @pl.when(to_back)
    def _():
        pl.semaphore_signal(barrier, 1, device_id=(down, after), device_id_type=MESH)

    fwd_route = (
        ((up, before), to_front, to_back),
        ((up, j), not_first_row, not_last_row),
        ((i, before), not_first_col, not_last_col),
    )
    back_route = (
        ((down, after), to_back, to_front),
        ((down, j), not_last_row, not_first_row),
        ((i, after), not_last_col, not_first_col),
    )
    quads = ((0, 0), (0, 1), (1, 0))
    counter = [0]
    pending = []

    def message(source, target, device, may_send):
        number = counter[0]
        counter[0] += 1
        copy = pltpu.make_async_remote_copy(
            source, target, send_sem.at[number], recv_sem.at[number],
            device_id=device, device_id_type=MESH,
        )
        if may_send is None:
            copy.start()
        else:
            pl.when(may_send)(lambda: copy.start())
        pending.append((copy, may_send))
        return copy

    def receive(copy, may_receive):
        if may_receive is None:
            copy.wait_recv()
        else:
            pl.when(may_receive)(lambda: copy.wait_recv())

    lane = lax.broadcasted_iota(jnp.int32, (HALF, SUB), 1)
    is_left = lane < HALF
    full_lane = lax.broadcasted_iota(jnp.int32, (SUB, SUB), 1)
    full_row = lax.broadcasted_iota(jnp.int32, (SUB, SUB), 0)
    tile_lane = lax.broadcasted_iota(jnp.int32, (8, SUB), 1)

    def swap(value):
        return pltpu.roll(value, HALF, 1)

    def send_quads(tiles, sender, receiver, route, apply, v):
        copies = []
        for q, (low, right) in enumerate(quads):
            span = slice(low * HALF, (low + 1) * HALF)
            for pair in range(TIERS // 2):
                first, second = tiles[pair][span], tiles[pair + TIERS // 2][span]
                if right:
                    packed = jnp.where(is_left, swap(first), second)
                else:
                    packed = jnp.where(is_left, first, swap(second))
                sender[apply, v, q, pair] = packed
            device, may_send, may_receive = route[q]
            copy = message(
                sender.at[apply, v, q], receiver.at[apply, v, q], device, may_send
            )
            copies.append((copy, may_receive))
        return copies

    def quad_halves(receiver, apply, v, t):
        pair, second = t % (TIERS // 2), t >= TIERS // 2
        top_left = receiver[apply, v, 0, pair]
        top_right = receiver[apply, v, 1, pair]
        low_left = receiver[apply, v, 2, pair]
        if second:
            top_left, low_left = swap(top_left), swap(low_left)
        else:
            top_right = swap(top_right)
        return jnp.where(is_left, top_left, top_right), low_left

    def right_mul(value, which):
        high, low = halves(value)
        wide = jnp.dot(
            jnp.concatenate([high, low], 1), rights[which], preferred_element_type=jnp.float32
        )
        return wide[:, :SUB] + wide[:, SUB:]

    def left_mul(value, which):
        high, low = halves(value)
        tall = jnp.dot(
            lefts[which], jnp.concatenate([high, low], 0), preferred_element_type=jnp.float32
        )
        return tall[:SUB] + tall[SUB:]

    def solve(tiles, plan):
        first = right_mul(jnp.concatenate(tiles, 0), plan[0])
        mid = []
        for t in range(TIERS):
            spectral = left_mul(first[t * SUB : (t + 1) * SUB], plan[1])
            mid.append(left_mul(spectral * inv_den[t], plan[2]))
        last = right_mul(jnp.concatenate(mid, 0), plan[3])
        return [last[t * SUB : (t + 1) * SUB] for t in range(TIERS)]

    def start_halo(number, tiles):
        west = jnp.zeros((SUB, SUB), jnp.float32)
        east = jnp.zeros((SUB, SUB), jnp.float32)
        for k, tile in enumerate(tiles):
            row_send[number, 0, k : k + 1, :] = tile[0:1]
            row_send[number, 1, k : k + 1, :] = tile[SUB - 1 : SUB]
            west = jnp.where(full_lane == k, pltpu.roll(tile, k, 1) if k else tile, west)
            east = jnp.where(full_lane == k, pltpu.roll(tile, k + 1, 1), east)
        col_send[number, 0] = west
        col_send[number, 1] = east
        return (
            (message(col_send.at[number, 0], col_recv.at[number, 1], (i, before), not_first_col), not_last_col),
            (message(col_send.at[number, 1], col_recv.at[number, 0], (i, after), not_last_col), not_first_col),
            (message(row_send.at[number, 0], row_recv.at[number, 1], (up, j), not_first_row), not_last_row),
            (message(row_send.at[number, 1], row_recv.at[number, 0], (down, j), not_last_row), not_first_row),
        )

    def neighbours(number, k, tile):
        north = jnp.where(full_row == 0, row_recv[number, 0, k : k + 1, :], pltpu.roll(tile, 1, 0))
        south = jnp.where(
            full_row == SUB - 1, row_recv[number, 1, k : k + 1, :], pltpu.roll(tile, SUB - 1, 0)
        )
        from_west = col_recv[number, 0]
        if k:
            from_west = pltpu.roll(from_west, SUB - k, 1)
        from_east = pltpu.roll(col_recv[number, 1], SUB - 1 - k, 1)
        west = jnp.where(full_lane == 0, from_west, pltpu.roll(tile, 1, 1))
        east = jnp.where(full_lane == SUB - 1, from_east, pltpu.roll(tile, SUB - 1, 1))
        return north, south, west, east

    def gather_start(number, parts):
        total = jnp.sum(jnp.concatenate(parts, 0), axis=1, keepdims=True)
        gather_cols[number, j] = jnp.broadcast_to(total, (8, SUB))
        return [
            message(
                gather_cols.at[number, j], gather_cols.at[number, j],
                (i, lax.rem(j + step, cols)), None,
            )
            for step in range(1, cols)
        ]

    def gather_middle(number, copies):
        for copy in copies:
            receive(copy, None)
        merged = jnp.zeros((8, SUB), jnp.float32)
        for c in range(cols):
            merged = jnp.where(tile_lane == c, gather_cols[number, c], merged)
        gather_rows[number, i] = merged
        return [
            message(
                gather_rows.at[number, i], gather_rows.at[number, i],
                (lax.rem(i + step, rows), j), None,
            )
            for step in range(1, rows)
        ]

    def gather_end(number, copies):
        for copy in copies:
            receive(copy, None)
        return [gather_rows[number, r] for r in range(rows)]

    for load in loads[:3]:
        load.wait()

    conds = []
    for t in range(TIERS):
        table = tier_table[t]
        ids = material[t]
        cond = jnp.zeros((SUB, SUB), jnp.float32)
        mean = 0.0
        mats = cond_table.shape[1]
        for m in range(mats):
            entry = cond_table[table, m]
            mean = mean + entry
            cond = jnp.where(ids == m, entry, cond)
        conds.append(cond)
        inv_mean = 1.0 / (jnp.full((8, SUB), mean, jnp.float32) * (1.0 / mats))
        inv_den[t] = recip[...] * inv_mean[0:1]

    for q in range(3):
        for route, receiver in ((fwd_route, fwd_recv), (back_route, back_recv)):

            @pl.when(jnp.logical_not(route[q][2]))
            def _():
                for apply in range(ITERS + 1):
                    for v in range(variants):
                        receiver[apply, v, q] = jnp.zeros(receiver.shape[3:], jnp.float32)

    for side, has_row, has_col in ((0, not_first_row, not_first_col), (1, not_last_row, not_last_col)):

        @pl.when(jnp.logical_not(has_row))
        def _():
            for number in range(ITERS * variants + 1):
                row_recv[number, side] = jnp.zeros((8, SUB), jnp.float32)

        @pl.when(jnp.logical_not(has_col))
        def _():
            for number in range(ITERS * variants + 1):
                col_recv[number, side] = jnp.zeros((SUB, SUB), jnp.float32)

    pl.semaphore_wait(
        barrier,
        cols - 1 + rows - 1 + to_front.astype(jnp.int32) + to_back.astype(jnp.int32),
    )

    def tile_sum(values):
        return jnp.sum(values, axis=0, keepdims=True)

    def start_apply(apply, get):
        return [
            send_quads(get(v), fwd_send, fwd_recv, fwd_route, apply, v) for v in range(variants)
        ]

    def residual_of(v):
        return [res[v, t] for t in range(TIERS)]

    forward = start_apply(0, residual_of)
    cond_halo = start_halo(0, conds)
    zero_row = jnp.zeros((1, SUB), jnp.float32)
    sums = [
        tile_sum(sum(residual_of(v)[1:], residual_of(v)[0])) * scale for v in range(variants)
    ]
    gather = gather_start(0, [zero_row] * 6 + sums)

    for load in loads[3:]:
        load.wait()
    mine = slots[i * cols + j]
    my_owner, my_place = lax.div(mine, own), lax.rem(mine, own)
    block = inverse[my_place]
    owner_lane = lax.broadcasted_iota(jnp.int32, block.shape, 1)
    entries = jnp.sum(jnp.where(owner_lane == my_owner, block, 0.0), axis=1, keepdims=True)
    weights = []
    row_lane = lax.broadcasted_iota(jnp.int32, (1, SUB), 1)
    for r in range(rows):
        places = jnp.full((1, SUB), -1, jnp.int32)
        for c in range(cols):
            places = jnp.where(row_lane == c, slots[r * cols + c] - my_owner * own, places)
        line = zero_row
        for k in range(own):
            line = jnp.where(places == k, entries[k : k + 1], line)
        weights.append(line)

    gather = gather_middle(0, gather)

    def coarse_of(coarse_state):
        mixed = weights[0] * coarse_state[0]
        for r in range(1, rows):
            mixed = mixed + weights[r] * coarse_state[r]
        return jnp.sum(mixed, axis=1, keepdims=True) * scale

    def solve_frames(apply, forward, own_low, update):
        backs = []
        for v in range(variants):
            for copy, may_receive in forward[v]:
                receive(copy, may_receive)
            frames = []
            for t in range(TIERS):
                top, low_left = quad_halves(fwd_recv, apply, v, t)
                low = jnp.where(is_left, low_left, own_low[v, t, HALF:, :])
                frames.append(update(v, t, jnp.concatenate([top, low], 0)))
            solved = solve(frames, (1, 2, 1, 2))
            backs.append(send_quads(solved, back_send, back_recv, back_route, apply, v))
            for t in range(TIERS):
                pre[v, t, HALF:, :] = jnp.where(is_left, 0.0, solved[t][HALF:])
        return backs

    def add_aligned(v, coarse):
        shift = coarse[6 + v : 7 + v]
        for t, tile in enumerate(solve(residual_of(v), (0, 0, 0, 0))):
            pre[v, t, :HALF, :] = tile[:HALF] + shift
            pre[v, t, HALF:, :] = pre[v, t, HALF:, :] + tile[HALF:] + shift

    def add_offset(apply, backs, v):
        for copy, may_receive in backs[v]:
            receive(copy, may_receive)
        for t in range(TIERS):
            top, low_left = quad_halves(back_recv, apply, v, t)
            pre[v, t, :HALF, :] = pre[v, t, :HALF, :] + top
            low = jnp.where(is_left, low_left, 0.0)
            pre[v, t, HALF:, :] = pre[v, t, HALF:, :] + low

    def halo_of(number, v):
        return 1 + number * variants + v

    def finish_apply(apply, backs, coarse):
        halos = []
        for v in range(variants):
            add_aligned(v, coarse)
        for v in range(variants):
            add_offset(apply, backs, v)
            if apply < ITERS:
                halos.append(start_halo(halo_of(apply, v), [pre[v, t] for t in range(TIERS)]))
        return halos

    def keep_frame(v, t, frame):
        frame_res[v, t] = frame
        return frame

    backs = solve_frames(0, forward, res, keep_frame)

    for copy, may_receive in cond_halo:
        receive(copy, may_receive)
    for t in range(TIERS):
        for side, other in enumerate(neighbours(0, t, conds[t])):
            coef[t, side] = 0.5 * (conds[t] + other)
        if t + 1 < TIERS:
            upward[t] = VERT_C * 0.5 * (conds[t] + conds[t + 1])
    sink[...] = SINK_C * conds[0]

    coarse_state = gather_end(0, gather)
    halos = finish_apply(0, backs, coarse_of(coarse_state))

    rz_old = curvature = coarse_image = None
    for number in range(ITERS):
        rz_parts, uw_parts, us_parts, q_parts, forward = [], [], [], [], []

        def apply_operator(v):
            for copy, may_receive in halos[v]:
                receive(copy, may_receive)
            rz_sum = uw_sum = us_sum = q_sum = zero_row
            for t in range(TIERS):
                tile = pre[v, t]
                out = None
                for side, other in enumerate(neighbours(halo_of(number, v), t, tile)):
                    term = coef[t, side] * (tile - other)
                    out = term if out is None else out + term
                if t + 1 < TIERS:
                    out = out + upward[t] * (tile - pre[v, t + 1])
                if t:
                    out = out - upward[t - 1] * (pre[v, t - 1] - tile)
                else:
                    out = out + sink[...] * tile
                image[v, t] = out
                rz_sum = rz_sum + tile_sum(res[v, t] * tile)
                uw_sum = uw_sum + tile_sum(out * tile)
                q_sum = q_sum + tile_sum(out)
                if number:
                    us_sum = us_sum + tile_sum(held_image[v, t] * tile)
            rz_parts.append(rz_sum)
            uw_parts.append(uw_sum)
            us_parts.append(us_sum)
            q_parts.append(q_sum * scale)

        def send_image(v):
            forward.append(
                send_quads(
                    [image[v, t] for t in range(TIERS)],
                    fwd_send, fwd_recv, fwd_route, number + 1, v,
                )
            )

        for v in range(variants):
            if v:
                send_image(v - 1)
            apply_operator(v)
        gather = gather_start(number + 1, rz_parts + uw_parts + us_parts + q_parts)
        send_image(variants - 1)
        gather = gather_middle(number + 1, gather)
        gathered = gather_end(number + 1, gather)
        total = gathered[0]
        for r in range(1, rows):
            total = total + gathered[r]
        total = jnp.broadcast_to(jnp.sum(total, axis=1, keepdims=True), (8, SUB))
        rz, uw, us = total[0:2], total[2:4], total[4:6]
        if number:
            beta = rz / rz_old
            curvature = uw + 2.0 * beta * us + beta * beta * curvature
        else:
            beta = None
            curvature = uw
        alpha = rz / curvature
        rz_old = rz

        def update_frame(v, t, frame):
            if number:
                frame = frame + beta[v : v + 1] * frame_image[v, t]
            if number + 1 < ITERS:
                frame_image[v, t] = frame
            updated = frame_res[v, t] - alpha[v : v + 1] * frame
            if number + 1 < ITERS:
                frame_res[v, t] = updated
            return updated

        for v in range(variants):
            step = alpha[v : v + 1]
            for t in range(TIERS):
                if number:
                    heading = pre[v, t] + beta[v : v + 1] * held[v, t]
                    sol[v, t] = sol[v, t] + step * heading
                else:
                    heading = pre[v, t]
                    sol[v, t] = step * heading
                if number + 1 < ITERS:
                    held[v, t] = heading
        backs = solve_frames(number + 1, forward, image, update_frame)
        for v in range(variants):
            step = alpha[v : v + 1]
            for t in range(TIERS):
                moved = image[v, t]
                if number:
                    moved = moved + beta[v : v + 1] * held_image[v, t]
                if number + 1 < ITERS:
                    held_image[v, t] = moved
                res[v, t] = res[v, t] - step * moved

        wide_alpha = jnp.concatenate([alpha] * 4, 0)
        if number:
            wide_beta = jnp.concatenate([beta] * 4, 0)
            coarse_image = [g + wide_beta * c for g, c in zip(gathered, coarse_image)]
        else:
            coarse_image = gathered
        coarse_state = [q - wide_alpha * c for q, c in zip(coarse_state, coarse_image)]
        halos = finish_apply(number + 1, backs, coarse_of(coarse_state))

    for copy, may_send in pending:
        if may_send is None:
            copy.wait_send()
        else:
            pl.when(may_send)(lambda copy=copy: copy.wait_send())


def write_out(*refs):
    count = len(refs) // 2
    sources, targets, sem = refs[:count], refs[count : 2 * count], refs[-1]
    copies = [
        pltpu.make_async_copy(source, target, sem.at[number])
        for number, (source, target) in enumerate(zip(sources, targets))
    ]
    for copy in copies:
        copy.start()
    for copy in copies:
        copy.wait()


def solution(mesh):
    rows, cols = mesh.shape["rows"], mesh.shape["cols"]
    rights, lefts, recip = split_constants()

    def shards(power, material, cond_table, tier_table, coarse_slot, coarse_inverse):
        variants = power.shape[0]
        owners, own = coarse_inverse.shape[:2]
        applies = ITERS + 1
        halos = ITERS * variants + 1
        messages = applies * variants * 6 + halos * 4 + applies * (rows - 1 + cols - 1)
        hbm = pl.BlockSpec(memory_space=pltpu.HBM)
        vmem = pl.BlockSpec(memory_space=pltpu.VMEM)
        smem = pl.BlockSpec(memory_space=pltpu.SMEM)
        field = (variants, TIERS, SUB, SUB)
        quad = (applies, variants, 3, TIERS // 2, HALF, SUB)

        def body(*refs):
            kernel(rows, cols, variants, owners, own, *refs)

        f32 = jnp.float32
        done = pl.pallas_call(
            body,
            out_shape=[pltpu.VMEM(power.shape, f32)] * 3,
            in_specs=[hbm] * 6 + [smem] * 3,
            out_specs=[vmem] * 3,
            scratch_shapes=[
                pltpu.VMEM((TIERS, SUB, SUB), jnp.int32),
                pltpu.VMEM(rights.shape, jnp.bfloat16),
                pltpu.VMEM(lefts.shape, jnp.bfloat16),
                pltpu.VMEM((SUB, SUB), f32),
                pltpu.VMEM((own, own, owners), f32),
                pltpu.VMEM(field, f32),
                pltpu.VMEM(field, f32),
                pltpu.VMEM((TIERS, SUB, SUB), f32),
                pltpu.VMEM((TIERS, 4, SUB, SUB), f32),
                pltpu.VMEM((TIERS - 1, SUB, SUB), f32),
                pltpu.VMEM((SUB, SUB), f32),
                pltpu.VMEM(field, f32),
                pltpu.VMEM(field, f32),
                pltpu.VMEM(field, f32),
                pltpu.VMEM(quad, f32),
                pltpu.VMEM(quad, f32),
                pltpu.VMEM(quad, f32),
                pltpu.VMEM(quad, f32),
                pltpu.VMEM((halos, 2, 8, SUB), f32),
                pltpu.VMEM((halos, 2, 8, SUB), f32),
                pltpu.VMEM((halos, 2, SUB, SUB), f32),
                pltpu.VMEM((halos, 2, SUB, SUB), f32),
                pltpu.VMEM((applies, cols, 8, SUB), f32),
                pltpu.VMEM((applies, rows, 8, SUB), f32),
                pltpu.SemaphoreType.DMA((messages,)),
                pltpu.SemaphoreType.DMA((messages,)),
                pltpu.SemaphoreType.DMA((6,)),
            ],
            compiler_params=pltpu.CompilerParams(
                collective_id=0, has_side_effects=True, vmem_limit_bytes=58 * 1024 * 1024
            ),
        )(
            power, material, jnp.asarray(rights), jnp.asarray(lefts), jnp.asarray(recip),
            jnp.transpose(coarse_inverse, (1, 2, 0)), cond_table, tier_table, coarse_slot,
        )
        return pl.pallas_call(
            write_out,
            out_shape=[jax.ShapeDtypeStruct(power.shape, f32)] * 3,
            in_specs=[vmem] * 3,
            out_specs=[hbm] * 3,
            scratch_shapes=[pltpu.SemaphoreType.DMA((3,))],
            compiler_params=pltpu.CompilerParams(vmem_limit_bytes=8 * 1024 * 1024),
        )(*done)

    in_specs = (P(None, None, "rows", "cols"), P(None, "rows", "cols"), P(), P(), P(), P())
    out_specs = (P(None, None, "rows", "cols"),) * 3
    return jax.shard_map(shards, mesh=mesh, in_specs=in_specs, out_specs=out_specs, check_vma=False)
```
